256 devices in a mesh: layer: 16 (over y_hi, x, core), latent: 16 (over z, y_lo).
Axes of the slice: x: 4, y: 4 (y_hi: 2, y_lo: 2; y = y_hi * 2 + y_lo), z: 8, core: 2. Of those that a mesh axis runs over, the one named last changes fastest.
Arguments:
- decoder: bfloat16 [65536, 4, 2304], P(('layer', 'latent')), may hold values from -0.375 to 0.375
- code_index: int32 [4, 128, 64], replicated, may hold values from 0 to 16383, all different within a row
- code_value: bfloat16 [4, 128, 64], replicated, may hold values from 0.19921875 to 4
- bias: float32 [4, 2304], replicated, may hold values from -3 to 3
- target: bfloat16 [4, 128, 2304], replicated, may hold values from -6 to 6
Outputs:
- layer_error: float32 [4], replicated
- grad_decoder: bfloat16 [65536, 4, 2304], P(('layer', 'latent'))
- code_grad: float32 [4, 128, 64], replicated
The draws below stay inside these ranges and needn't reach their ends.
Inputs may be any that keep to these rules, and one draw needn't show every extreme that they name: `code_index`: the 64 indices of one token in one layer are distinct.
All inputs are finite; a program needn't handle non-finite values.
Results may differ from the reference program's by a relative error of at most 0.0048.
Values may be sent and summed in bfloat16 or wider, within the bound.
A program may use at most 64 MiB of HBM per device.

```python
import math
import jax
import jax.numpy as jnp
from jax import lax

D = 2304
F = 16384
LAYERS = 4
TOPK = 64
TOKENS = 128


def shard_levels(own_key, shape, pieces, low, high):
    factor_of = 1.0
    for dim, shards_of in pieces:
        steps = jax.random.uniform(jax.random.fold_in(jax.random.fold_in(own_key, 6), dim), (shards_of,), jnp.float32, low / len(pieces), high / len(pieces))
        factor_of = factor_of * jnp.repeat(jnp.exp(steps), shape[dim] // shards_of).reshape((-1,) + (1,) * (len(shape) - 1 - dim))
    return factor_of


def choose_distinct(key, rows, count, top, lift):
    order = jax.random.permutation(jax.random.fold_in(key, 1), count)
    boost = order
    for power in range(3):
        boost = boost * boost // count
    boost = boost * lift // count
    lots = jax.random.randint(jax.random.fold_in(key, 2), (rows, count), 0, 4096) + boost
    sure = jax.random.permutation(jax.random.fold_in(key, 3), rows)[jnp.arange(count) % rows]
    lots = jnp.where(jnp.arange(rows)[:, None] == sure[None, :], 1 << 14, lots)
    merit = lots * count + jnp.arange(count)
    return lax.top_k(merit.astype(jnp.int32), top)[1].astype(jnp.int32)


def normal_values(key, extent, deviation, limit, pieces=(), held_as=jnp.bfloat16):
    drawn = jax.random.normal(key, extent, jnp.float32) * deviation
    if len(pieces) > 0:
        drawn = shard_levels(key, extent, pieces, -0.22, 0.18) * drawn
    return jnp.clip(drawn, min=-limit, max=limit).astype(held_as)


def setup_inputs(seed: int = 0) -> dict:
    key_of = jax.random.split(jax.random.key(seed), 6)
    decoder = normal_values(key_of[0], (LAYERS * F, LAYERS, D), (LAYERS * TOPK) ** -0.5, 0.375, ((0, 256),))
    code_index = choose_distinct(key_of[1], LAYERS * TOKENS, F, TOPK, 32).reshape((LAYERS, TOKENS, TOPK))
    code_value = jnp.clip(jnp.exp(jax.random.uniform(key_of[2], (LAYERS, TOKENS, TOPK), jnp.float32, math.log(0.19921875), math.log(4.0))), 0.19921875, 4.0).astype(jnp.bfloat16)
    bias = normal_values(key_of[3], (LAYERS, D), 0.5, 3.0, (), jnp.float32)
    target = normal_values(key_of[4], (LAYERS, TOKENS, D), 1.0, 6.0)
    return {"decoder": decoder, "code_index": code_index, "code_value": code_value, "bias": bias, "target": target}


def reference(decoder, code_index, code_value, bias, target):
    token_count = code_index.shape[1]
    token_rows = jnp.arange(token_count, dtype=jnp.int32)[:, None]
    dense_codes = []
    for src_layer in range(LAYERS):
        filled = jnp.zeros((token_count, F), jnp.float32).at[token_rows, code_index[src_layer]].add(code_value[src_layer].astype(jnp.float32))
        dense_codes.append(filled.astype(jnp.bfloat16))
    errors = []
    for tgt_layer in range(LAYERS):
        recon_sum = jnp.zeros((token_count, D), jnp.float32)
        for src_layer in range(tgt_layer + 1):
            weight_slab = decoder[src_layer * F:(src_layer + 1) * F, tgt_layer, :]
            recon_sum = recon_sum + jnp.dot(dense_codes[src_layer], weight_slab, preferred_element_type=jnp.float32)
        errors.append(recon_sum + bias[tgt_layer][None, :] - target[tgt_layer].astype(jnp.float32))
    residual = jnp.stack(errors)
    layer_error = jnp.mean(residual * residual, axis=(1, 2))
    error_b = residual.astype(jnp.bfloat16)
    grad_rows = []
    code_grads = []
    for src_layer in range(LAYERS):
        blocks = []
        code_sums = jnp.zeros((token_count, F), jnp.float32)
        for tgt_layer in range(LAYERS):
            if tgt_layer < src_layer:
                blocks.append(jnp.zeros((F, D), jnp.bfloat16))
            else:
                weight_slab = decoder[src_layer * F:(src_layer + 1) * F, tgt_layer, :]
                blocks.append(jnp.dot(dense_codes[src_layer].T, error_b[tgt_layer], preferred_element_type=jnp.float32).astype(jnp.bfloat16))
                code_sums = code_sums + jnp.dot(error_b[tgt_layer], weight_slab.T, preferred_element_type=jnp.float32)
        grad_rows.append(jnp.stack(blocks, axis=1))
        code_grads.append(jnp.take_along_axis(code_sums, code_index[src_layer], axis=1))
    return layer_error, jnp.concatenate(grad_rows, axis=0), jnp.stack(code_grads)
```

```python
import jax
import jax.numpy as jnp
from jax import lax
from jax.experimental import pallas as pl
from jax.experimental.pallas import tpu as pltpu
from jax.sharding import Mesh
from jax.sharding import PartitionSpec as P

D = 2304
LAYERS = 4
TOPK = 64
TOKENS = 128
SLAB = 256
TILE = 128
PAIRS = D // (2 * TILE)
GROUPS = 3
WIDE = PAIRS // GROUPS
HALF = TOKENS // 2
ROWS = 16
AXES = ("yh", "x", "core", "z", "yl")
MESH = pl.DeviceIdType.MESH
f32 = jnp.float32
bf16 = jnp.bfloat16


def contract(left, right, left_dim, right_dim):
    return lax.dot_general(
        left, right, (((left_dim,), (right_dim,)), ((), ())), preferred_element_type=f32
    )


def here():
    x, core, z = lax.axis_index("x"), lax.axis_index("core"), lax.axis_index("z")
    y = lax.axis_index("yh") * 2 + lax.axis_index("yl")
    return x, y, z, core


def source_layer():
    return lax.axis_index("yh") * 2 + lax.axis_index("x") // 2


def at_x(x):
    return {"x": x}


def at_y(y):
    return {"yh": y // 2, "yl": lax.rem(y, 2)}


def at_z(z):
    return {"z": z}


def slot_of(x, y, core):
    return ((y // 2) * 2 + x // 2) * 8 + lax.rem(y, 2) * 4 + lax.rem(x, 2) * 2 + core


def remote(src, dst, sems, index, device):
    return pltpu.make_async_remote_copy(
        src_ref=src,
        dst_ref=dst,
        send_sem=sems[0].at[index],
        recv_sem=sems[1].at[index],
        device_id=device,
        device_id_type=MESH,
    )


def loop(low, high, body):
    def step(i, carry):
        body(i)
        return carry

    lax.fori_loop(low, high, step, 0)


def exchange_kernel(
    decoder, index_ref, value_ref, bias_ref, target,
    error_out, codes_out, grad_out, square_out,
    weights, spread_codes, forward, own, core_send, core_recv, own_b, target_v,
    recv1, sum1, sum1_b, recv2, sum2, sum2_b, recv3,
    error, squares, square_recv, products, sums, picked, pick_recv, message, plane, gathered,
    weight_sem, target_sem, error_sem,
    core_s, core_r, one_s, one_r, two_s, two_r, three_s, three_r,
    az_s, az_r, sq_s, sq_r, as_s, as_r, af_s, af_r, ac_s, ac_r,
    pz_s, pz_r, pp_s, pp_r, pa_s, pa_r,
):
    x, y, z, core = here()
    source = source_layer()
    offset = ((lax.rem(x, 2) * 2 + core) * 16 + z * 2 + lax.axis_index("yl")) * SLAB
    other = {"core": 1 - core}
    first, second = (x, y), (y, x)
    at_first, at_second = (at_x, at_y), (at_y, at_x)
    tokens_of = [pl.multiple_of(core * HALF + first[p] * ROWS, ROWS) for p in range(2)]

    def weight_copy(tile):
        return pltpu.make_async_copy(
            decoder.at[:, :, pl.ds(tile * TILE, TILE)], weights.at[tile], weight_sem.at[tile]
        )

    def target_copy(p, which):
        tile = (z if which == 0 else PAIRS - 1) * 2 + p
        columns = pl.ds(pl.multiple_of(tile * TILE, TILE), TILE)
        return pltpu.make_async_copy(
            target.at[second[p], pl.ds(tokens_of[p], ROWS), columns],
            target_v.at[p, which],
            target_sem.at[p, which],
        )

    for tile in range(2 * PAIRS):
        weight_copy(tile).start()
    for p in range(2):
        for which in range(2):
            target_copy(p, which).start()

    barrier = pltpu.get_barrier_semaphore()

    def plane_peer(j, sign):
        px = lax.rem(x + 4 + sign * lax.rem(j, 4), 4)
        py = lax.rem(y + 4 + sign * lax.rem(j // 4, 4), 4)
        return px, py, lax.rem(core + j // 16, 2)

    def at_plane(j):
        px, py, pc = plane_peer(j, 1)
        return {"x": px, "core": pc, **at_y(py)}

    def z_peer(i):
        return lax.rem(z + i, 8)

    loop(1, 32, lambda j: pl.semaphore_signal(barrier, inc=1, device_id=at_plane(j), device_id_type=MESH))
    loop(1, 8, lambda i: pl.semaphore_signal(barrier, inc=1, device_id=at_z(z_peer(i)), device_id_type=MESH))

    latents = lax.broadcasted_iota(jnp.int32, (SLAB, TOKENS), 0)

    def place(i, dense):
        part = pl.ds(pl.multiple_of(i * ROWS, ROWS), ROWS)
        columns = index_ref[source, part, :] - offset
        values = value_ref[source, part, :].astype(f32)
        for k in range(ROWS):
            dense = jnp.where(latents == columns[k : k + 1, :], values[k : k + 1, :], dense)
        return dense

    dense = lax.fori_loop(0, TOPK // ROWS, place, jnp.zeros((SLAB, TOKENS), f32)).astype(bf16)
    codes_out[...] = dense
    lane = lax.broadcasted_iota(jnp.int32, (SLAB, LAYERS * SLAB), 1)
    row = lax.broadcasted_iota(jnp.int32, (SLAB, LAYERS * SLAB), 0)
    spread = jnp.where((lane >> 2) == row, 1.0, 0.0).astype(bf16)
    spread_codes[...] = contract(dense, spread, 0, 0)
    lane = lax.broadcasted_iota(jnp.int32, (HALF, LAYERS * SLAB), 1) & 3
    for side in range(2):
        half = spread_codes[pl.ds(pl.multiple_of((core if side == 0 else 1 - core) * HALF, HALF), HALF), :]
        for t in range(LAYERS):
            kept = jnp.where(jnp.logical_and(lane == t, t >= source), half, 0.0)
            forward[(side * LAYERS + t) * HALF : (side * LAYERS + t + 1) * HALF, :] = kept.astype(bf16)

    flat = weights.reshape(2 * PAIRS, LAYERS * SLAB, TILE)

    def core_copy(g):
        part = pl.ds(g * WIDE, WIDE)
        return remote(core_send.at[part], core_recv.at[part], (core_s, core_r), g, other)

    def one_copy(g, p, i):
        part = pl.ds(g * WIDE, WIDE)
        k = lax.rem(first[p] + i, 4)
        rows = pl.ds(pl.multiple_of(k * ROWS, ROWS), ROWS)
        return remote(
            own_b.at[part, p, :, rows, :], recv1.at[p, i - 1, part],
            (one_s, one_r), (p, g, i - 1), at_first[p](k),
        )

    def two_copy(g, p, i):
        part = pl.ds(g * WIDE, WIDE)
        k = lax.rem(second[p] + i, 4)
        return remote(
            sum1_b.at[p, part, k], recv2.at[p, i - 1, part],
            (two_s, two_r), (p, g, i - 1), at_second[p](k),
        )

    def three_copy(p, which, i):
        k = z_peer(i)
        return remote(
            sum2_b.at[p, k if which == 0 else PAIRS - 1], recv3.at[p, i - 1, which],
            (three_s, three_r), (p, which, i - 1), at_z(k),
        )

    def after_core(g):
        core_copy(g).wait_recv()

        def add(i):
            b, p = g * WIDE + i // 2, lax.rem(i, 2)
            total = own[b, p] + core_recv[b, p].astype(f32)
            own[b, p] = total
            own_b[b, p] = total.astype(bf16)

        loop(0, 2 * WIDE, add)
        for i in range(1, 4):
            for p in range(2):
                one_copy(g, p, i).start()

    for g in range(GROUPS):
        for b in range(g * WIDE, (g + 1) * WIDE):
            weight_copy(2 * b).wait()
            weight_copy(2 * b + 1).wait()
            product = contract(forward[...], jnp.concatenate([flat[2 * b], flat[2 * b + 1]], axis=1), 1, 0)
            for p in range(2):
                columns = slice(p * TILE, (p + 1) * TILE)
                own[b, p] = product[: LAYERS * HALF, columns].reshape(LAYERS, HALF, TILE)
                core_send[b, p] = product[LAYERS * HALF :, columns].reshape(LAYERS, HALF, TILE).astype(bf16)
        if g == 0:
            pl.semaphore_wait(barrier, 38)
        core_copy(g).start()
        if g > 0:
            after_core(g - 1)
    after_core(GROUPS - 1)

    for g in range(GROUPS):
        for p in range(2):
            for i in range(1, 4):
                one_copy(g, p, i).wait_recv()

            def add(b):
                total = own[b, p, :, pl.ds(pl.multiple_of(first[p] * ROWS, ROWS), ROWS), :]
                for i in range(3):
                    total = total + recv1[p, i, b].astype(f32)
                sum1[p, b] = total
                sum1_b[p, b] = total.astype(bf16)

            loop(g * WIDE, (g + 1) * WIDE, add)
            for i in range(1, 4):
                two_copy(g, p, i).start()

    for g in range(GROUPS):
        for p in range(2):
            for i in range(1, 4):
                two_copy(g, p, i).wait_recv()

            def add(b):
                total = sum1[p, b, second[p]]
                for i in range(3):
                    total = total + recv2[p, i, b].astype(f32)
                sum2[p, b] = total
                sum2_b[p, b] = total.astype(bf16)

            loop(g * WIDE, (g + 1) * WIDE, add)

    def send_three(i):
        for p in range(2):
            for which in range(2):
                three_copy(p, which, i).start()

    loop(1, 8, send_three)

    tile_row = lax.broadcasted_iota(jnp.int32, (8, TILE), 0)
    layer_row = lax.broadcasted_iota(jnp.int32, (LAYERS, TILE), 0)
    squared = jnp.zeros((8, TILE), f32)

    def z_copy(p, i):
        tile = error.at[z, p, second[p], pl.ds(tokens_of[p], ROWS), :]
        return remote(tile, tile, (az_s, az_r), (p, i - 1), at_z(z_peer(i)))

    def square_copy(i):
        return remote(squares, square_recv.at[z], (sq_s, sq_r), i - 1, at_z(z_peer(i)))

    for p in range(2):
        for which in range(2):
            loop(1, 8, lambda i: three_copy(p, which, i).wait_recv())
            target_copy(p, which).wait()
            tile = z if which == 0 else PAIRS - 1
            total = sum2[p, tile]
            for i in range(7):
                total = total + recv3[p, i, which].astype(f32)
            columns = pl.ds(pl.multiple_of((tile * 2 + p) * TILE, TILE), TILE)
            shift = jnp.sum(jnp.where(layer_row == second[p], bias_ref[:, columns], 0.0), axis=0, keepdims=True)
            residual = total + shift - target_v[p, which].astype(f32)
            error[tile, p, second[p], pl.ds(tokens_of[p], ROWS), :] = residual.astype(bf16)
            square = jnp.sum(residual * residual, axis=0, keepdims=True)
            counted = tile_row == second[p]
            if which == 1:
                counted = jnp.logical_and(counted, z == 0)
            squared = squared + jnp.where(counted, square, 0.0)
            if which == 0:
                loop(1, 8, lambda i: z_copy(p, i).start())
    squares[...] = squared
    square_recv[z] = squared
    loop(1, 8, lambda i: square_copy(i).start())

    def second_copy(p, i):
        tiles = error.at[:, p, second[p], pl.ds(tokens_of[p], ROWS), :]
        return remote(tiles, tiles, (as_s, as_r), (p, i - 1), at_second[p](lax.rem(second[p] + i, 4)))

    def first_copy(g, p, i):
        tiles = error.at[pl.ds(g * WIDE, WIDE), p, :, pl.ds(tokens_of[p], ROWS), :]
        return remote(tiles, tiles, (af_s, af_r), (p, g, i - 1), at_first[p](lax.rem(first[p] + i, 4)))

    def half_copy(g):
        tiles = error.at[pl.ds(g * WIDE, WIDE), :, :, pl.ds(pl.multiple_of(core * HALF, HALF), HALF), :]
        return remote(tiles, tiles, (ac_s, ac_r), g, other)

    def error_copy(g):
        part = pl.ds(g * WIDE, WIDE)
        return pltpu.make_async_copy(error.at[part], error_out.at[part], error_sem.at[g])

    for p in range(2):
        loop(1, 8, lambda i: z_copy(p, i).wait_recv())
        for i in range(1, 4):
            second_copy(p, i).start()
    for p in range(2):
        for i in range(1, 4):
            second_copy(p, i).wait_recv()
    for g in range(GROUPS):
        for i in range(1, 4):
            for p in range(2):
                first_copy(g, p, i).start()
    for g in range(GROUPS):
        for p in range(2):
            for i in range(1, 4):
                first_copy(g, p, i).wait_recv()
        half_copy(g).start()
        if g > 0:
            backward(g - 1, half_copy, error_copy, flat, error, products)
    backward(GROUPS - 1, half_copy, error_copy, flat, error, products)

    total = jnp.zeros((SLAB, TOKENS), f32)
    for t in range(LAYERS):
        total = total + jnp.where(t >= source, products[t, pl.ds(t, SLAB, stride=LAYERS), :], 0.0)
    sums[...] = total
    columns = index_ref[source] - offset

    def pick(i, out):
        rows = sums[pl.ds(pl.multiple_of(i * 8, 8), 8), :]
        for r in range(8):
            out = jnp.where(columns == i * 8 + r, rows[r : r + 1, :], out)
        return out

    picked[...] = lax.fori_loop(0, SLAB // 8, pick, jnp.zeros((TOPK, TOKENS), f32))

    def pick_copy(i):
        k = z_peer(i)
        rows = picked.at[pl.ds(pl.multiple_of(k * 8, 8), 8), :]
        return remote(rows, pick_recv.at[i - 1], (pz_s, pz_r), i - 1, at_z(k))

    my_slot = slot_of(x, y, core)
    z_rows = pl.ds(pl.multiple_of(z * 8, 8), 8)

    def plane_copy(j):
        return remote(message, plane.at[my_slot], (pp_s, pp_r), j - 1, at_plane(j))

    def plane_arrival(j):
        return remote(message, plane.at[slot_of(*plane_peer(j, -1))], (pp_s, pp_r), j - 1, at_plane(j))

    def gather_copy(i):
        rows = gathered.at[:, z_rows, :]
        return remote(rows, rows, (pa_s, pa_r), i - 1, at_z(z_peer(i)))

    loop(1, 8, lambda i: pick_copy(i).start())
    loop(1, 8, lambda i: square_copy(i).wait_recv())
    total = square_recv[0]
    for i in range(1, 8):
        total = total + square_recv[i]
    message[1] = total
    loop(1, 8, lambda i: pick_copy(i).wait_recv())
    total = picked[z_rows, :]
    for i in range(7):
        total = total + pick_recv[i]
    message[0] = total
    plane[my_slot] = message[...]
    loop(1, 32, lambda j: plane_copy(j).start())
    loop(1, 32, lambda j: plane_arrival(j).wait_recv())
    squared = jnp.zeros((8, TILE), f32)
    for s in range(LAYERS):
        total = plane[s * 8, 0]
        squared = squared + plane[s * 8, 1]
        for i in range(1, 8):
            total = total + plane[s * 8 + i, 0]
            squared = squared + plane[s * 8 + i, 1]
        gathered[s, z_rows, :] = total
    loop(1, 8, lambda i: gather_copy(i).start())
    square_out[...] = squared

    for g in range(GROUPS):
        core_copy(g).wait_send()
        half_copy(g).wait_send()
        error_copy(g).wait()
        for p in range(2):
            for i in range(1, 4):
                one_copy(g, p, i).wait_send()
                two_copy(g, p, i).wait_send()
                first_copy(g, p, i).wait_send()
    for p in range(2):
        for i in range(1, 4):
            second_copy(p, i).wait_send()

    def z_sent(i):
        for p in range(2):
            z_copy(p, i).wait_send()
            for which in range(2):
                three_copy(p, which, i).wait_send()
        square_copy(i).wait_send()
        pick_copy(i).wait_send()

    loop(1, 8, z_sent)
    loop(1, 32, lambda j: plane_copy(j).wait_send())
    loop(1, 8, lambda i: gather_copy(i).wait())
    grad_out[...] = gathered[...]


def backward(g, half_copy, error_copy, flat, error, products):
    half_copy(g).wait_recv()
    error_copy(g).start()
    left, right = [], []
    for b in range(g * WIDE, (g + 1) * WIDE):
        for p in range(2):
            left.append(flat[2 * b + p])
            right.append(error[b, p].reshape(LAYERS * TOKENS, TILE))
    product = contract(jnp.concatenate(left, axis=1), jnp.concatenate(right, axis=1), 1, 1)
    for t in range(LAYERS):
        block = product[:, t * TILE : (t + 1) * TILE]
        products[t] = block if g == 0 else products[t] + block


def grads_kernel(codes_ref, error_ref, grads, spread, staged, sems):
    source = source_layer()
    row = lax.broadcasted_iota(jnp.int32, (LAYERS * SLAB, SLAB), 0)
    lane = lax.broadcasted_iota(jnp.int32, (LAYERS * SLAB, SLAB), 1)
    pattern = jnp.where((row >> 2) == lane, 1.0, 0.0).astype(bf16)
    wide = contract(pattern, codes_ref[...], 1, 0)
    row = lax.broadcasted_iota(jnp.int32, (LAYERS * SLAB, TOKENS), 0) & 3
    for t in range(LAYERS):
        kept = jnp.where(jnp.logical_and(row == t, t >= source), wide, 0.0)
        spread[:, t * TOKENS : (t + 1) * TOKENS] = kept.astype(bf16)
    flat = staged.reshape(2 * PAIRS, LAYERS * SLAB, TILE)

    def out_copy(tile):
        return pltpu.make_async_copy(
            staged.at[tile], grads.at[:, :, pl.ds(tile * TILE, TILE)], sems.at[tile]
        )

    for b in range(PAIRS):
        both = [error_ref[b, p].reshape(LAYERS * TOKENS, TILE) for p in range(2)]
        product = contract(spread[...], jnp.concatenate(both, axis=1), 1, 0).astype(bf16)
        for p in range(2):
            flat[2 * b + p] = product[:, p * TILE : (p + 1) * TILE]
            out_copy(2 * b + p).start()
    for tile in range(2 * PAIRS):
        out_copy(tile).wait()


def on_device(decoder, code_index, code_value, bias, target):
    in_vmem = pl.BlockSpec(memory_space=pltpu.VMEM)
    anywhere = pl.BlockSpec(memory_space=pl.ANY)

    def shape(*dims):
        return lambda dtype: pltpu.VMEM(dims, dtype)

    def sems(*dims):
        return pltpu.SemaphoreType.DMA(dims)

    errors = (PAIRS, 2, LAYERS, TOKENS, TILE)
    error_b, codes, grad, squares = pl.pallas_call(
        exchange_kernel,
        name="exchange",
        out_shape=(
            jax.ShapeDtypeStruct(errors, bf16),
            jax.ShapeDtypeStruct((SLAB, TOKENS), bf16),
            jax.ShapeDtypeStruct((LAYERS, TOPK, TOKENS), f32),
            jax.ShapeDtypeStruct((8, TILE), f32),
        ),
        in_specs=[anywhere, in_vmem, in_vmem, in_vmem, anywhere],
        out_specs=(anywhere, in_vmem, in_vmem, in_vmem),
        scratch_shapes=[
            pltpu.VMEM((2 * PAIRS, SLAB, LAYERS, TILE), bf16),
            pltpu.VMEM((TOKENS, LAYERS * SLAB), f32),
            pltpu.VMEM((LAYERS * TOKENS, LAYERS * SLAB), bf16),
            pltpu.VMEM((PAIRS, 2, LAYERS, HALF, TILE), f32),
            pltpu.VMEM((PAIRS, 2, LAYERS, HALF, TILE), bf16),
            pltpu.VMEM((PAIRS, 2, LAYERS, HALF, TILE), bf16),
            pltpu.VMEM((PAIRS, 2, LAYERS, HALF, TILE), bf16),
            pltpu.VMEM((2, 2, ROWS, TILE), bf16),
            pltpu.VMEM((2, 3, PAIRS, LAYERS, ROWS, TILE), bf16),
            pltpu.VMEM((2, PAIRS, LAYERS, ROWS, TILE), f32),
            pltpu.VMEM((2, PAIRS, LAYERS, ROWS, TILE), bf16),
            pltpu.VMEM((2, 3, PAIRS, ROWS, TILE), bf16),
            pltpu.VMEM((2, PAIRS, ROWS, TILE), f32),
            pltpu.VMEM((2, PAIRS, ROWS, TILE), bf16),
            pltpu.VMEM((2, 7, 2, ROWS, TILE), bf16),
            pltpu.VMEM(errors, bf16),
            pltpu.VMEM((8, TILE), f32),
            pltpu.VMEM((8, 8, TILE), f32),
            pltpu.VMEM((LAYERS, LAYERS * SLAB, TOKENS), f32),
            pltpu.VMEM((SLAB, TOKENS), f32),
            pltpu.VMEM((TOPK, TOKENS), f32),
            pltpu.VMEM((7, 8, TILE), f32),
            pltpu.VMEM((2, 8, TILE), f32),
            pltpu.VMEM((32, 2, 8, TILE), f32),
            pltpu.VMEM((LAYERS, TOPK, TOKENS), f32),
            sems(2 * PAIRS), sems(2, 2), sems(GROUPS),
            sems(GROUPS), sems(GROUPS), sems(2, GROUPS, 3), sems(2, GROUPS, 3),
            sems(2, GROUPS, 3), sems(2, GROUPS, 3), sems(2, 2, 7), sems(2, 2, 7),
            sems(2, 7), sems(2, 7), sems(7), sems(7), sems(2, 3), sems(2, 3),
            sems(2, GROUPS, 3), sems(2, GROUPS, 3), sems(GROUPS), sems(GROUPS),
            sems(7), sems(7), sems(31), sems(31), sems(7), sems(7),
        ],
        compiler_params=pltpu.CompilerParams(
            collective_id=0, has_side_effects=True, vmem_limit_bytes=44 << 20
        ),
    )(
        decoder,
        jnp.transpose(code_index, (0, 2, 1)),
        jnp.transpose(code_value, (0, 2, 1)),
        bias,
        target,
    )
    grads = pl.pallas_call(
        grads_kernel,
        name="decoder_gradient",
        out_shape=jax.ShapeDtypeStruct(decoder.shape, bf16),
        in_specs=[in_vmem, in_vmem],
        out_specs=anywhere,
        scratch_shapes=[
            pltpu.VMEM((LAYERS * SLAB, LAYERS * TOKENS), bf16),
            pltpu.VMEM((2 * PAIRS, SLAB, LAYERS, TILE), bf16),
            sems(2 * PAIRS),
        ],
        compiler_params=pltpu.CompilerParams(vmem_limit_bytes=32 << 20),
    )(codes, error_b)
    layer_error = jnp.sum(squares[:LAYERS], axis=1) / (TOKENS * D)
    return layer_error, grads, jnp.transpose(grad, (0, 2, 1))


def solution(mesh):
    torus = Mesh(mesh.devices.reshape(2, 4, 2, 8, 2), AXES)
    rows = P(AXES, None, None)
    return jax.shard_map(
        on_device,
        mesh=torus,
        in_specs=(rows, P(), P(), P(), P()),
        out_specs=(P(), rows, P()),
        check_vma=False,
    )
```

```python
import functools

import jax
import jax.numpy as jnp
from jax import lax
from jax.experimental import pallas as pl
from jax.experimental.pallas import tpu as pltpu
from jax.sharding import Mesh
from jax.sharding import PartitionSpec as P

D = 2304
LAYERS = 4
TOPK = 64
TOKENS = 128
SLAB = 256
TILE = 128
PAIRS = D // (2 * TILE)
GROUPS = 3
WIDE = PAIRS // GROUPS
HALF = TOKENS // 2
ROWS = 16
AXES = ("yh", "x", "core", "z", "yl")
MESH = pl.DeviceIdType.MESH
f32 = jnp.float32
bf16 = jnp.bfloat16


def contract(left, right, left_dim, right_dim):
    return lax.dot_general(
        left, right, (((left_dim,), (right_dim,)), ((), ())), preferred_element_type=f32
    )


def here():
    x, core, z = lax.axis_index("x"), lax.axis_index("core"), lax.axis_index("z")
    y = lax.axis_index("yh") * 2 + lax.axis_index("yl")
    return x, y, z, core


def source_layer():
    return lax.axis_index("yh") * 2 + lax.axis_index("x") // 2


def at_x(x):
    return {"x": x}


def at_y(y):
    return {"yh": y // 2, "yl": lax.rem(y, 2)}


def at_z(z):
    return {"z": z}


def remote(src, dst, sems, index, device):
    return pltpu.make_async_remote_copy(
        src_ref=src,
        dst_ref=dst,
        send_sem=sems[0].at[index],
        recv_sem=sems[1].at[index],
        device_id=device,
        device_id_type=MESH,
    )


def waits(low, high, copy):
    return lambda: loop(low, high, lambda i: copy(i).wait_send())


def loop(low, high, body):
    def step(i, carry):
        body(i)
        return carry

    lax.fori_loop(low, high, step, 0)


def exchange_kernel(
    decoder, index_hbm, value_hbm, bias_hbm, target,
    grads_out, grad_out, square_out,
    weights, index_ref, value_ref, bias_ref, spread_codes, forward, own, core_send, core_recv, own_b, target_v,
    recv1, sum1, sum1_b, recv2, sum2, sum2_b, recv3,
    error, codes, wide_codes, squares, products, sums, picked, pick_recv, by_z, by_plane,
    small_sem, weight_sem, target_sem,
    core_s, core_r, one_s, one_r, two_s, two_r, three_s, three_r,
    as_s, as_r, af_s, af_r, ac_s, ac_r,
    az_s, az_r, pn_s, pn_r, pz_s, pz_r, pp_s, pp_r, pc_s, pc_r,
):
    x, y, z, core = here()
    source = source_layer()
    offset = ((lax.rem(x, 2) * 2 + core) * 16 + z * 2 + lax.axis_index("yl")) * SLAB
    other = {"core": 1 - core}
    pending = []
    first, second = (x, y), (y, x)
    at_first, at_second = (at_x, at_y), (at_y, at_x)
    tokens_of = [pl.multiple_of(core * HALF + first[p] * ROWS, ROWS) for p in range(2)]

    def group(g):
        return pl.ds(g * WIDE, WIDE)

    def weight_copy(tile):
        return pltpu.make_async_copy(
            decoder.at[:, :, pl.ds(tile * TILE, TILE)], weights.at[tile], weight_sem.at[tile]
        )

    def target_copy(p, which):
        tile = (z if which == 0 else PAIRS - 1) * 2 + p
        columns = pl.ds(pl.multiple_of(tile * TILE, TILE), TILE)
        return pltpu.make_async_copy(
            target.at[second[p], pl.ds(tokens_of[p], ROWS), columns],
            target_v.at[p, which],
            target_sem.at[p, which],
        )

    barrier = pltpu.get_barrier_semaphore()

    def z_peer(i):
        return lax.rem(z + i, 8)

    def at_plane(i):
        return {"x": lax.rem(x + lax.rem(i, 4), 4), **at_y(lax.rem(y + i // 4, 4))}

    def flip(position, by):
        return position + by * (1 - 2 * lax.rem(position, 2))

    def near(i):
        return flip(x, lax.rem(i, 2)), flip(y, lax.rem(i // 2, 2)), flip(core, i // 4)

    def at_near(i):
        px, py, pc = near(i)
        return {"x": px, "core": pc, **at_y(py)}

    def greet(device):
        pl.semaphore_signal(barrier, inc=1, device_id=device, device_id_type=MESH)

    loop(1, 8, lambda i: greet(at_z(z_peer(i))))
    loop(1, 16, lambda i: greet(at_plane(i)))
    loop(4, 8, lambda i: greet(at_near(i)))

    small = [
        pltpu.make_async_copy(index_hbm.at[source], index_ref, small_sem.at[0]),
        pltpu.make_async_copy(value_hbm.at[source], value_ref, small_sem.at[1]),
        pltpu.make_async_copy(bias_hbm, bias_ref, small_sem.at[2]),
    ]
    for copy in small:
        copy.start()
    for tile in range(2 * PAIRS):
        weight_copy(tile).start()
    for p in range(2):
        for which in range(2):
            target_copy(p, which).start()

    for copy in small:
        copy.wait()
    latents = lax.broadcasted_iota(jnp.int32, (SLAB, TOKENS), 0)

    def place(i, dense):
        part = pl.ds(pl.multiple_of(i * ROWS, ROWS), ROWS)
        columns = index_ref[part, :] - offset
        values = value_ref[part, :].astype(f32)
        for k in range(ROWS):
            dense = jnp.where(latents == columns[k : k + 1, :], values[k : k + 1, :], dense)
        return dense

    dense = lax.fori_loop(0, TOPK // ROWS, place, jnp.zeros((SLAB, TOKENS), f32)).astype(bf16)
    codes[...] = dense
    lane = lax.broadcasted_iota(jnp.int32, (SLAB, LAYERS * SLAB), 1)
    row = lax.broadcasted_iota(jnp.int32, (SLAB, LAYERS * SLAB), 0)
    spread = jnp.where((lane >> 2) == row, 1.0, 0.0).astype(bf16)
    spread_codes[...] = contract(dense, spread, 0, 0)
    lane = lax.broadcasted_iota(jnp.int32, (HALF, LAYERS * SLAB), 1) & 3
    for side in range(2):
        half = spread_codes[pl.ds(pl.multiple_of((core if side == 0 else 1 - core) * HALF, HALF), HALF), :]
        for t in range(LAYERS):
            kept = jnp.where(jnp.logical_and(lane == t, t >= source), half, 0.0)
            forward[(side * LAYERS + t) * HALF : (side * LAYERS + t + 1) * HALF, :] = kept.astype(bf16)

    flat = weights.reshape(2 * PAIRS, LAYERS * SLAB, TILE)

    def core_copy(g):
        return remote(core_send.at[group(g)], core_recv.at[group(g)], (core_s, core_r), g, other)

    def one_copy(g, p, i):
        k = lax.rem(first[p] + i, 4)
        rows = pl.ds(pl.multiple_of(k * ROWS, ROWS), ROWS)
        return remote(
            own_b.at[group(g), p, :, rows, :], recv1.at[p, i - 1, group(g)],
            (one_s, one_r), (p, g, i - 1), at_first[p](k),
        )

    def two_copy(g, p, i):
        k = lax.rem(second[p] + i, 4)
        return remote(
            sum1_b.at[p, group(g), k], recv2.at[p, i - 1, group(g)],
            (two_s, two_r), (p, g, i - 1), at_second[p](k),
        )

    def three_copy(p, which, i):
        k = z_peer(i)
        return remote(
            sum2_b.at[p, k if which == 0 else PAIRS - 1], recv3.at[p, i - 1, which],
            (three_s, three_r), (p, which, i - 1), at_z(k),
        )

    def z_copy(p, i):
        tile = error.at[z, p, second[p], pl.ds(tokens_of[p], ROWS), :]
        return remote(tile, tile, (az_s, az_r), (p, i - 1), at_z(z_peer(i)))

    def second_copy(p, i):
        tiles = error.at[:, p, second[p], pl.ds(tokens_of[p], ROWS), :]
        return remote(tiles, tiles, (as_s, as_r), (p, i - 1), at_second[p](lax.rem(second[p] + i, 4)))

    def first_copy(g, p, i):
        tiles = error.at[group(g), p, :, pl.ds(tokens_of[p], ROWS), :]
        return remote(tiles, tiles, (af_s, af_r), (p, g, i - 1), at_first[p](lax.rem(first[p] + i, 4)))

    def half_copy(g):
        tiles = error.at[group(g), :, :, pl.ds(pl.multiple_of(core * HALF, HALF), HALF), :]
        return remote(tiles, tiles, (ac_s, ac_r), g, other)

    def exchange(copy, g):
        for i in range(1, 4):
            for p in range(2):
                copy(g, p, i).start()
                pending.append(copy(g, p, i).wait_send)

    def arrive(copy, g):
        for p in range(2):
            for i in range(1, 4):
                copy(g, p, i).wait_recv()

    def add_core(g):
        core_copy(g).wait_recv()

        def add(i):
            b, p = g * WIDE + i // 2, lax.rem(i, 2)
            total = own[b, p] + core_recv[b, p].astype(f32)
            own[b, p] = total
            own_b[b, p] = total.astype(bf16)

        loop(0, 2 * WIDE, add)
        exchange(one_copy, g)

    def add_first(g):
        arrive(one_copy, g)
        for p in range(2):

            def add(b):
                total = own[b, p, :, pl.ds(pl.multiple_of(first[p] * ROWS, ROWS), ROWS), :]
                for i in range(3):
                    total = total + recv1[p, i, b].astype(f32)
                sum1[p, b] = total
                sum1_b[p, b] = total.astype(bf16)

            loop(g * WIDE, (g + 1) * WIDE, add)
        exchange(two_copy, g)

    def add_second(g):
        arrive(two_copy, g)
        for p in range(2):

            def add(b):
                total = sum1[p, b, second[p]]
                for k in range(3):
                    total = total + recv2[p, k, b].astype(f32)
                sum2[p, b] = total
                sum2_b[p, b] = total.astype(bf16)

            loop(g * WIDE, (g + 1) * WIDE, add)

    def add_z():
        def send(i):
            for p in range(2):
                for which in range(2):
                    three_copy(p, which, i).start()

        loop(1, 8, send)
        pending.extend(waits(1, 8, functools.partial(three_copy, p, which)) for p in range(2) for which in range(2))

    layer_row = lax.broadcasted_iota(jnp.int32, (LAYERS, TILE), 0)
    tile_row = lax.broadcasted_iota(jnp.int32, (8, TILE), 0)

    def take_errors():
        squared = jnp.zeros((8, TILE), f32)
        for which in range(2):
            for p in range(2):
                loop(1, 8, lambda i: three_copy(p, which, i).wait_recv())
                target_copy(p, which).wait()
                tile = z if which == 0 else PAIRS - 1
                total = sum2[p, tile]
                for i in range(7):
                    total = total + recv3[p, i, which].astype(f32)
                columns = pl.ds(pl.multiple_of((tile * 2 + p) * TILE, TILE), TILE)
                shift = jnp.sum(jnp.where(layer_row == second[p], bias_ref[:, columns], 0.0), axis=0, keepdims=True)
                residual = total + shift - target_v[p, which].astype(f32)
                error[tile, p, second[p], pl.ds(tokens_of[p], ROWS), :] = residual.astype(bf16)
                if which == 0:
                    loop(1, 8, lambda i: z_copy(p, i).start())
                    pending.append(waits(1, 8, functools.partial(z_copy, p)))
                square = jnp.sum(residual * residual, axis=0, keepdims=True)
                counted = tile_row == second[p]
                if which == 1:
                    counted = jnp.logical_and(counted, z == 0)
                squared = squared + jnp.where(counted, square, 0.0)
        squares[...] = squared

    def pass_layers():
        for p in range(2):
            loop(1, 8, lambda i: z_copy(p, i).wait_recv())
            for i in range(1, 4):
                second_copy(p, i).start()
                pending.append(second_copy(p, i).wait_send)
        for p in range(2):
            for i in range(1, 4):
                second_copy(p, i).wait_recv()

    def pass_rows(g):
        arrive(first_copy, g)
        half_copy(g).start()
        pending.append(half_copy(g).wait_send)

    def backward(g):
        half_copy(g).wait_recv()
        left, right = [], []
        for b in range(g * WIDE, (g + 1) * WIDE):
            for p in range(2):
                left.append(flat[2 * b + p])
                right.append(error[b, p].reshape(LAYERS * TOKENS, TILE))
        product = contract(jnp.concatenate(left, axis=1), jnp.concatenate(right, axis=1), 1, 1)
        for t in range(LAYERS):
            block = product[:, t * TILE : (t + 1) * TILE]
            products[t] = block if g == 0 else products[t] + block

    def project(g):
        for tile in range(2 * g * WIDE, 2 * (g + 1) * WIDE):
            weight_copy(tile).wait()
        for b in range(g * WIDE, (g + 1) * WIDE):
            product = contract(forward[...], jnp.concatenate([flat[2 * b], flat[2 * b + 1]], axis=1), 1, 0)
            for p in range(2):
                columns = slice(p * TILE, (p + 1) * TILE)
                own[b, p] = product[: LAYERS * HALF, columns].reshape(LAYERS, HALF, TILE)
                core_send[b, p] = product[LAYERS * HALF :, columns].reshape(LAYERS, HALF, TILE).astype(bf16)

    def send_core(g):
        core_copy(g).start()
        pending.append(core_copy(g).wait_send)

    project(0)
    project(1)
    pl.semaphore_wait(barrier, 26)
    send_core(0)
    send_core(1)
    project(2)
    send_core(2)
    for stage in (add_core, add_first, add_second):
        for g in range(GROUPS):
            stage(g)
    add_z()
    pattern_row = lax.broadcasted_iota(jnp.int32, (LAYERS * SLAB, SLAB), 0)
    pattern_lane = lax.broadcasted_iota(jnp.int32, (LAYERS * SLAB, SLAB), 1)
    pattern = jnp.where((pattern_row >> 2) == pattern_lane, 1.0, 0.0).astype(bf16)
    tall = contract(pattern, codes[...], 1, 0)
    pattern_row = lax.broadcasted_iota(jnp.int32, (LAYERS * SLAB, TOKENS), 0) & 3
    for t in range(LAYERS):
        kept = jnp.where(jnp.logical_and(pattern_row == t, t >= source), tall, 0.0)
        wide_codes[:, t * TOKENS : (t + 1) * TOKENS] = kept.astype(bf16)
    take_errors()
    pass_layers()
    for g in range(GROUPS):
        exchange(first_copy, g)
    for g in range(GROUPS):
        pass_rows(g)
        if g > 0:
            backward(g - 1)
    backward(GROUPS - 1)

    total = jnp.zeros((SLAB, TOKENS), f32)
    for t in range(LAYERS):
        total = total + jnp.where(t >= source, products[t, pl.ds(t, SLAB, stride=LAYERS), :], 0.0)
    sums[...] = total
    columns = index_ref[...] - offset

    def pick(i, out):
        rows = sums[pl.ds(pl.multiple_of(i * 8, 8), 8), :]
        for r in range(8):
            out = jnp.where(columns == i * 8 + r, rows[r : r + 1, :], out)
        return out

    picked[...] = lax.fori_loop(0, SLAB // 8, pick, jnp.zeros((TOPK, TOKENS), f32))

    flat_out = grads_out.reshape(2 * PAIRS, LAYERS * SLAB, TILE)

    def decoder_gradients(g):
        for b in range(g * WIDE, (g + 1) * WIDE):
            both = [error[b, p].reshape(LAYERS * TOKENS, TILE) for p in range(2)]
            product = contract(wide_codes[...], jnp.concatenate(both, axis=1), 1, 0).astype(bf16)
            for p in range(2):
                flat_out[2 * b + p] = product[:, p * TILE : (p + 1) * TILE]

    def rank(px, py, pc):
        return lax.rem(px, 2) + 2 * lax.rem(py, 2) + 4 * pc

    def near_copy(i):
        rows = picked.at[pl.ds(pl.multiple_of(rank(*near(i)) * 8, 8), 8), :]
        return remote(rows, pick_recv.at[i - 1], (pn_s, pn_r), i - 1, at_near(i))

    def sum_copy(i):
        return remote(by_z.at[z], by_z.at[z], (pz_s, pz_r), i - 1, at_z(z_peer(i)))

    def plane_copy(i):
        mine = by_plane.at[core, y * 4 + x]
        return remote(mine, mine, (pp_s, pp_r), i - 1, at_plane(i))

    def pair_copy():
        return remote(by_plane.at[core], by_plane.at[core], (pc_s, pc_r), 0, other)

    loop(1, 8, lambda i: near_copy(i).start())
    pending.append(waits(1, 8, near_copy))
    decoder_gradients(0)
    loop(1, 8, lambda i: near_copy(i).wait_recv())
    total = picked[pl.ds(pl.multiple_of(rank(x, y, core) * 8, 8), 8), :]
    for i in range(7):
        total = total + pick_recv[i]
    by_z[z, 0] = total
    by_z[z, 1] = squares[...]
    loop(1, 8, lambda i: sum_copy(i).start())
    pending.append(waits(1, 8, sum_copy))
    decoder_gradients(1)
    loop(1, 8, lambda i: sum_copy(i).wait_recv())
    total = by_z[0]
    for i in range(1, 8):
        total = total + by_z[i]
    by_plane[core, y * 4 + x] = total
    loop(1, 16, lambda i: plane_copy(i).start())
    pending.append(waits(1, 16, plane_copy))
    decoder_gradients(2)
    loop(1, 16, lambda i: plane_copy(i).wait_recv())
    pair_copy().start()
    pending.append(pair_copy().wait_send)
    for wait in pending[:-1]:
        wait()
    pair_copy().wait_recv()
    squared = jnp.zeros((8, TILE), f32)
    for pc in range(2):
        for py in range(4):
            for px in range(4):
                at = (px % 2 + 2 * (py % 2) + 4 * pc) * 8
                grad_out[py // 2 * 2 + px // 2, at : at + 8, :] = by_plane[pc, py * 4 + px, 0]
                squared = squared + by_plane[pc, py * 4 + px, 1]
    square_out[...] = squared
    pending[-1]()


def layout_kernel(grads, out, sems):
    copies = [
        pltpu.make_async_copy(grads.at[tile], out.at[:, :, pl.ds(tile * TILE, TILE)], sems.at[tile])
        for tile in range(2 * PAIRS)
    ]
    for copy in copies:
        copy.start()
    for copy in copies:
        copy.wait()


def on_device(decoder, code_index, code_value, bias, target):
    in_vmem = pl.BlockSpec(memory_space=pltpu.VMEM)
    in_hbm = pl.BlockSpec(memory_space=pltpu.HBM)

    def sems(*dims):
        return pltpu.SemaphoreType.DMA(dims)

    errors = (PAIRS, 2, LAYERS, TOKENS, TILE)
    staged, grad, squares = pl.pallas_call(
        exchange_kernel,
        name="exchange",
        out_shape=(
            pltpu.VMEM((2 * PAIRS, SLAB, LAYERS, TILE), bf16),
            jax.ShapeDtypeStruct((LAYERS, TOPK, TOKENS), f32),
            jax.ShapeDtypeStruct((8, TILE), f32),
        ),
        in_specs=[in_hbm] * 5,
        out_specs=(in_vmem, in_vmem, in_vmem),
        scratch_shapes=[
            pltpu.VMEM((2 * PAIRS, SLAB, LAYERS, TILE), bf16),
            pltpu.VMEM((TOPK, TOKENS), jnp.int32),
            pltpu.VMEM((TOPK, TOKENS), bf16),
            pltpu.VMEM((LAYERS, D), f32),
            pltpu.VMEM((TOKENS, LAYERS * SLAB), f32),
            pltpu.VMEM((LAYERS * TOKENS, LAYERS * SLAB), bf16),
            pltpu.VMEM((PAIRS, 2, LAYERS, HALF, TILE), f32),
            pltpu.VMEM((PAIRS, 2, LAYERS, HALF, TILE), bf16),
            pltpu.VMEM((PAIRS, 2, LAYERS, HALF, TILE), bf16),
            pltpu.VMEM((PAIRS, 2, LAYERS, HALF, TILE), bf16),
            pltpu.VMEM((2, 2, ROWS, TILE), bf16),
            pltpu.VMEM((2, 3, PAIRS, LAYERS, ROWS, TILE), bf16),
            pltpu.VMEM((2, PAIRS, LAYERS, ROWS, TILE), f32),
            pltpu.VMEM((2, PAIRS, LAYERS, ROWS, TILE), bf16),
            pltpu.VMEM((2, 3, PAIRS, ROWS, TILE), bf16),
            pltpu.VMEM((2, PAIRS, ROWS, TILE), f32),
            pltpu.VMEM((2, PAIRS, ROWS, TILE), bf16),
            pltpu.VMEM((2, 7, 2, ROWS, TILE), bf16),
            pltpu.VMEM(errors, bf16),
            pltpu.VMEM((SLAB, TOKENS), bf16),
            pltpu.VMEM((LAYERS * SLAB, LAYERS * TOKENS), bf16),
            pltpu.VMEM((8, TILE), f32),
            pltpu.VMEM((LAYERS, LAYERS * SLAB, TOKENS), f32),
            pltpu.VMEM((SLAB, TOKENS), f32),
            pltpu.VMEM((TOPK, TOKENS), f32),
            pltpu.VMEM((7, 8, TILE), f32),
            pltpu.VMEM((8, 2, 8, TILE), f32),
            pltpu.VMEM((2, 16, 2, 8, TILE), f32),
            sems(3), sems(2 * PAIRS), sems(2, 2),
            sems(GROUPS), sems(GROUPS), sems(2, GROUPS, 3), sems(2, GROUPS, 3),
            sems(2, GROUPS, 3), sems(2, GROUPS, 3), sems(2, 2, 7), sems(2, 2, 7),
            sems(2, 3), sems(2, 3), sems(2, GROUPS, 3), sems(2, GROUPS, 3),
            sems(GROUPS), sems(GROUPS), sems(2, 7), sems(2, 7),
            sems(7), sems(7), sems(7), sems(7), sems(15), sems(15), sems(1), sems(1),
        ],
        compiler_params=pltpu.CompilerParams(
            collective_id=0, has_side_effects=True, vmem_limit_bytes=40 << 20
        ),
    )(
        *[
            pltpu.with_memory_space_constraint(array, pltpu.HBM)
            for array in (
                decoder,
                jnp.transpose(code_index, (0, 2, 1)),
                jnp.transpose(code_value, (0, 2, 1)),
                bias,
                target,
            )
        ]
    )
    grads = pl.pallas_call(
        layout_kernel,
        name="decoder_gradient",
        out_shape=jax.ShapeDtypeStruct(decoder.shape, bf16),
        in_specs=[in_vmem],
        out_specs=in_hbm,
        scratch_shapes=[sems(2 * PAIRS)],
        compiler_params=pltpu.CompilerParams(vmem_limit_bytes=8 << 20),
    )(pltpu.with_memory_space_constraint(staged, pltpu.VMEM))
    layer_error = jnp.sum(squares[:LAYERS], axis=1) / (TOKENS * D)
    return layer_error, grads, jnp.transpose(grad, (0, 2, 1))


def solution(mesh):
    torus = Mesh(mesh.devices.reshape(2, 4, 2, 8, 2), AXES)
    rows = P(AXES, None, None)
    return jax.shard_map(
        on_device,
        mesh=torus,
        in_specs=(rows, P(), P(), P(), P()),
        out_specs=(P(), rows, P()),
        check_vma=False,
    )
```

```python
import functools

import jax
import jax.numpy as jnp
from jax import lax
from jax.experimental import pallas as pl
from jax.experimental.pallas import tpu as pltpu
from jax.sharding import Mesh
from jax.sharding import PartitionSpec as P

D = 2304
LAYERS = 4
TOPK = 64
TOKENS = 128
SLAB = 256
TILE = 128
PAIRS = D // (2 * TILE)
GROUPS = 3
WIDE = PAIRS // GROUPS
HALF = TOKENS // 2
ROWS = 16
AXES = ("yh", "x", "core", "z", "yl")
MESH = pl.DeviceIdType.MESH
f32 = jnp.float32
bf16 = jnp.bfloat16


def contract(left, right, left_dim, right_dim):
    return lax.dot_general(
        left, right, (((left_dim,), (right_dim,)), ((), ())), preferred_element_type=f32
    )


def here():
    x, core, z = lax.axis_index("x"), lax.axis_index("core"), lax.axis_index("z")
    y = lax.axis_index("yh") * 2 + lax.axis_index("yl")
    return x, y, z, core


def source_layer():
    return lax.axis_index("yh") * 2 + lax.axis_index("x") // 2


def at_x(x):
    return {"x": x}


def at_y(y):
    return {"yh": y // 2, "yl": lax.rem(y, 2)}


def at_z(z):
    return {"z": z}


def remote(src, dst, sems, index, device):
    return pltpu.make_async_remote_copy(
        src_ref=src,
        dst_ref=dst,
        send_sem=sems[0].at[index],
        recv_sem=sems[1].at[index],
        device_id=device,
        device_id_type=MESH,
    )


def waits(low, high, copy):
    return lambda: loop(low, high, lambda i: copy(i).wait_send())


def loop(low, high, body):
    def step(i, carry):
        body(i)
        return carry

    lax.fori_loop(low, high, step, 0)


def exchange_kernel(
    decoder, index_hbm, value_hbm, bias_hbm, target,
    grads_out, grad_out, square_out,
    weights, index_ref, value_ref, bias_ref, spread_codes, forward, own, core_send, core_recv, own_b, target_v,
    recv1, sum1, sum1_b, recv2, sum2, send3, recv3,
    error, by_z_error, codes, wide_codes, squares, products, sums, picked, pick_recv, by_z, by_plane,
    small_sem, weight_sem, target_sem,
    core_s, core_r, one_s, one_r, two_s, two_r, three_s, three_r,
    as_s, as_r, af_s, af_r, ac_s, ac_r,
    az_s, az_r, pn_s, pn_r, pz_s, pz_r, pp_s, pp_r, pc_s, pc_r,
):
    x, y, z, core = here()
    source = source_layer()
    offset = ((lax.rem(x, 2) * 2 + core) * 16 + z * 2 + lax.axis_index("yl")) * SLAB
    other = {"core": 1 - core}
    pending = []
    first, second = (x, y), (y, x)
    at_first, at_second = (at_x, at_y), (at_y, at_x)
    tokens_of = [pl.multiple_of(core * HALF + first[p] * ROWS, ROWS) for p in range(2)]

    def group(g):
        return pl.ds(g * WIDE, WIDE)

    def weight_copy(tile):
        return pltpu.make_async_copy(
            decoder.at[:, :, pl.ds(tile * TILE, TILE)], weights.at[tile], weight_sem.at[tile]
        )

    def target_copy(p, which):
        tile = (z if which == 0 else PAIRS - 1) * 2 + p
        columns = pl.ds(pl.multiple_of(tile * TILE, TILE), TILE)
        return pltpu.make_async_copy(
            target.at[second[p], pl.ds(tokens_of[p], ROWS), columns],
            target_v.at[p, which],
            target_sem.at[p, which],
        )

    small = [
        pltpu.make_async_copy(index_hbm.at[source], index_ref, small_sem.at[0]),
        pltpu.make_async_copy(value_hbm.at[source], value_ref, small_sem.at[1]),
        pltpu.make_async_copy(bias_hbm, bias_ref, small_sem.at[2]),
    ]
    for copy in small:
        copy.start()
    for tile in range(2 * PAIRS):
        weight_copy(tile).start()
    for p in range(2):
        for which in range(2):
            target_copy(p, which).start()

    barrier = pltpu.get_barrier_semaphore()

    def z_peer(i):
        return lax.rem(z + i, 8)

    def at_plane(i):
        return {"x": lax.rem(x + lax.rem(i, 4), 4), **at_y(lax.rem(y + i // 4, 4))}

    def flip(position, by):
        return position + by * (1 - 2 * lax.rem(position, 2))

    def near(i):
        return flip(x, lax.rem(i, 2)), flip(y, lax.rem(i // 2, 2)), flip(core, i // 4)

    def at_near(i):
        px, py, pc = near(i)
        return {"x": px, "core": pc, **at_y(py)}

    def greet(device):
        pl.semaphore_signal(barrier, inc=1, device_id=device, device_id_type=MESH)

    loop(1, 8, lambda i: greet(at_z(z_peer(i))))
    loop(1, 16, lambda i: greet(at_plane(i)))
    loop(4, 8, lambda i: greet(at_near(i)))

    for copy in small:
        copy.wait()
    latents = lax.broadcasted_iota(jnp.int32, (SLAB, TOKENS), 0)

    def place(i, dense):
        part = pl.ds(pl.multiple_of(i * ROWS, ROWS), ROWS)
        columns = index_ref[part, :] - offset
        values = value_ref[part, :].astype(f32)
        for k in range(ROWS):
            dense = jnp.where(latents == columns[k : k + 1, :], values[k : k + 1, :], dense)
        return dense

    dense = lax.fori_loop(0, TOPK // ROWS, place, jnp.zeros((SLAB, TOKENS), f32)).astype(bf16)
    codes[...] = dense
    lane = lax.broadcasted_iota(jnp.int32, (SLAB, LAYERS * SLAB), 1)
    row = lax.broadcasted_iota(jnp.int32, (SLAB, LAYERS * SLAB), 0)
    spread = jnp.where((lane >> 2) == row, 1.0, 0.0).astype(bf16)
    spread_codes[...] = contract(dense, spread, 0, 0)
    lane = lax.broadcasted_iota(jnp.int32, (HALF, LAYERS * SLAB), 1) & 3
    for side in range(2):
        half = spread_codes[pl.ds(pl.multiple_of((core if side == 0 else 1 - core) * HALF, HALF), HALF), :]
        for t in range(LAYERS):
            kept = jnp.where(jnp.logical_and(lane == t, t >= source), half, 0.0)
            forward[(side * LAYERS + t) * HALF : (side * LAYERS + t + 1) * HALF, :] = kept.astype(bf16)

    flat = weights.reshape(2 * PAIRS, LAYERS * SLAB, TILE)

    def core_copy(g):
        return remote(core_send.at[group(g)], core_recv.at[group(g)], (core_s, core_r), g, other)

    def one_copy(g, p, i):
        k = lax.rem(first[p] + i, 4)
        rows = pl.ds(pl.multiple_of(k * ROWS, ROWS), ROWS)
        return remote(
            own_b.at[group(g), p, :, rows, :], recv1.at[p, i - 1, group(g)],
            (one_s, one_r), (p, g, i - 1), at_first[p](k),
        )

    def two_copy(g, p, i):
        k = lax.rem(second[p] + i, 4)
        return remote(
            sum1_b.at[p, group(g), k], recv2.at[p, i - 1, group(g)],
            (two_s, two_r), (p, g, i - 1), at_second[p](k),
        )

    def three_copy(i):
        return remote(send3.at[z_peer(i)], recv3.at[i - 1], (three_s, three_r), i - 1, at_z(z_peer(i)))

    def z_copy(i):
        return remote(by_z_error.at[z], by_z_error.at[z], (az_s, az_r), i - 1, at_z(z_peer(i)))

    def second_copy(p, i):
        tiles = error.at[:, p, second[p], pl.ds(tokens_of[p], ROWS), :]
        return remote(tiles, tiles, (as_s, as_r), (p, i - 1), at_second[p](lax.rem(second[p] + i, 4)))

    def first_copy(g, p, i):
        tiles = error.at[group(g), p, :, pl.ds(tokens_of[p], ROWS), :]
        return remote(tiles, tiles, (af_s, af_r), (p, g, i - 1), at_first[p](lax.rem(first[p] + i, 4)))

    def half_copy(g):
        tiles = error.at[group(g), :, :, pl.ds(pl.multiple_of(core * HALF, HALF), HALF), :]
        return remote(tiles, tiles, (ac_s, ac_r), g, other)

    def exchange(copy, g):
        for i in range(1, 4):
            for p in range(2):
                copy(g, p, i).start()
                pending.append(copy(g, p, i).wait_send)

    def arrive(copy, g):
        for p in range(2):
            for i in range(1, 4):
                copy(g, p, i).wait_recv()

    def add_core(g):
        core_copy(g).wait_recv()

        def add(i):
            b, p = g * WIDE + i // 2, lax.rem(i, 2)
            total = own[b, p] + core_recv[b, p].astype(f32)
            own[b, p] = total
            own_b[b, p] = total.astype(bf16)

        loop(0, 2 * WIDE, add)
        exchange(one_copy, g)

    def add_first(g):
        arrive(one_copy, g)
        for p in range(2):

            def add(b):
                total = own[b, p, :, pl.ds(pl.multiple_of(first[p] * ROWS, ROWS), ROWS), :]
                for i in range(3):
                    total = total + recv1[p, i, b].astype(f32)
                sum1[p, b] = total
                sum1_b[p, b] = total.astype(bf16)

            loop(g * WIDE, (g + 1) * WIDE, add)
        exchange(two_copy, g)

    def add_second(g):
        arrive(two_copy, g)
        for p in range(2):

            for b in range(g * WIDE, (g + 1) * WIDE):
                total = sum1[p, b, second[p]]
                for k in range(3):
                    total = total + recv2[p, k, b].astype(f32)
                sum2[p, b] = total
                if b < 8:
                    send3[b, 0, p] = total.astype(bf16)
                else:
                    for k in range(8):
                        send3[k, 1, p] = total.astype(bf16)

    def add_z():
        loop(1, 8, lambda i: three_copy(i).start())
        pending.append(waits(1, 8, three_copy))

    layer_row = lax.broadcasted_iota(jnp.int32, (LAYERS, TILE), 0)
    tile_row = lax.broadcasted_iota(jnp.int32, (8, TILE), 0)

    def take_errors():
        squared = jnp.zeros((8, TILE), f32)
        loop(1, 8, lambda i: three_copy(i).wait_recv())
        for which in range(2):
            for p in range(2):
                target_copy(p, which).wait()
                tile = z if which == 0 else PAIRS - 1
                total = sum2[p, tile]
                for i in range(7):
                    total = total + recv3[i, which, p].astype(f32)
                columns = pl.ds(pl.multiple_of((tile * 2 + p) * TILE, TILE), TILE)
                shift = jnp.sum(jnp.where(layer_row == second[p], bias_ref[:, columns], 0.0), axis=0, keepdims=True)
                residual = total + shift - target_v[p, which].astype(f32)
                if which == 0:
                    by_z_error[z, p] = residual.astype(bf16)
                else:
                    error[tile, p, second[p], pl.ds(tokens_of[p], ROWS), :] = residual.astype(bf16)
                square = jnp.sum(residual * residual, axis=0, keepdims=True)
                counted = tile_row == second[p]
                if which == 1:
                    counted = jnp.logical_and(counted, z == 0)
                squared = squared + jnp.where(counted, square, 0.0)
            if which == 0:
                loop(1, 8, lambda i: z_copy(i).start())
                pending.append(waits(1, 8, z_copy))
        squares[...] = squared

    def pass_layers():
        loop(1, 8, lambda i: z_copy(i).wait_recv())
        for p in range(2):
            for b in range(8):
                error[b, p, second[p], pl.ds(tokens_of[p], ROWS), :] = by_z_error[b, p]
            for i in range(1, 4):
                second_copy(p, i).start()
                pending.append(second_copy(p, i).wait_send)
        for p in range(2):
            for i in range(1, 4):
                second_copy(p, i).wait_recv()

    def pass_rows(g):
        arrive(first_copy, g)
        half_copy(g).start()
        pending.append(half_copy(g).wait_send)

    def backward(g):
        half_copy(g).wait_recv()
        left, right = [], []
        for b in range(g * WIDE, (g + 1) * WIDE):
            for p in range(2):
                left.append(flat[2 * b + p])
                right.append(error[b, p].reshape(LAYERS * TOKENS, TILE))
        product = contract(jnp.concatenate(left, axis=1), jnp.concatenate(right, axis=1), 1, 1)
        for t in range(LAYERS):
            block = product[:, t * TILE : (t + 1) * TILE]
            products[t] = block if g == 0 else products[t] + block

    def project(g):
        for tile in range(2 * g * WIDE, 2 * (g + 1) * WIDE):
            weight_copy(tile).wait()
        tiles = [flat[tile] for tile in range(2 * g * WIDE, 2 * (g + 1) * WIDE)]
        product = contract(forward[...], jnp.concatenate(tiles, axis=1), 1, 0)
        for i in range(WIDE):
            b = g * WIDE + i
            for p in range(2):
                columns = slice((2 * i + p) * TILE, (2 * i + p + 1) * TILE)
                own[b, p] = product[: LAYERS * HALF, columns].reshape(LAYERS, HALF, TILE)
                core_send[b, p] = product[LAYERS * HALF :, columns].reshape(LAYERS, HALF, TILE).astype(bf16)

    def send_core(g):
        core_copy(g).start()
        pending.append(core_copy(g).wait_send)

    project(0)
    project(1)
    pl.semaphore_wait(barrier, 26)
    send_core(0)
    send_core(1)
    project(2)
    send_core(2)
    for stage in (add_core, add_first, add_second):
        for g in range(GROUPS):
            stage(g)
    add_z()
    pattern_row = lax.broadcasted_iota(jnp.int32, (LAYERS * SLAB, SLAB), 0)
    pattern_lane = lax.broadcasted_iota(jnp.int32, (LAYERS * SLAB, SLAB), 1)
    pattern = jnp.where((pattern_row >> 2) == pattern_lane, 1.0, 0.0).astype(bf16)
    tall = contract(pattern, codes[...], 1, 0)
    pattern_row = lax.broadcasted_iota(jnp.int32, (LAYERS * SLAB, TOKENS), 0) & 3
    for t in range(LAYERS):
        kept = jnp.where(jnp.logical_and(pattern_row == t, t >= source), tall, 0.0)
        wide_codes[:, t * TOKENS : (t + 1) * TOKENS] = kept.astype(bf16)
    take_errors()
    pass_layers()
    for g in range(GROUPS):
        exchange(first_copy, g)
    for g in range(GROUPS):
        pass_rows(g)
        if g > 0:
            backward(g - 1)
    backward(GROUPS - 1)

    total = jnp.zeros((SLAB, TOKENS), f32)
    for t in range(LAYERS):
        total = total + jnp.where(t >= source, products[t, pl.ds(t, SLAB, stride=LAYERS), :], 0.0)
    sums[...] = total
    columns = index_ref[...] - offset

    def pick(i, out):
        rows = sums[pl.ds(pl.multiple_of(i * 8, 8), 8), :]
        for r in range(8):
            out = jnp.where(columns == i * 8 + r, rows[r : r + 1, :], out)
        return out

    picked[...] = lax.fori_loop(0, SLAB // 8, pick, jnp.zeros((TOPK, TOKENS), f32))

    flat_out = grads_out.reshape(2 * PAIRS, LAYERS * SLAB, TILE)

    def decoder_gradients(g):
        tiles = range(2 * g * WIDE, 2 * (g + 1) * WIDE)
        errors = [error[tile // 2, tile % 2].reshape(LAYERS * TOKENS, TILE) for tile in tiles]
        product = contract(wide_codes[...], jnp.concatenate(errors, axis=1), 1, 0).astype(bf16)
        for i, tile in enumerate(tiles):
            flat_out[tile] = product[:, i * TILE : (i + 1) * TILE]

    def rank(px, py, pc):
        return lax.rem(px, 2) + 2 * lax.rem(py, 2) + 4 * pc

    def near_copy(i):
        rows = picked.at[pl.ds(pl.multiple_of(rank(*near(i)) * 8, 8), 8), :]
        return remote(rows, pick_recv.at[i - 1], (pn_s, pn_r), i - 1, at_near(i))

    def sum_copy(i):
        return remote(by_z.at[z], by_z.at[z], (pz_s, pz_r), i - 1, at_z(z_peer(i)))

    def plane_copy(i):
        mine = by_plane.at[core, y * 4 + x]
        return remote(mine, mine, (pp_s, pp_r), i - 1, at_plane(i))

    def pair_copy():
        return remote(by_plane.at[core], by_plane.at[core], (pc_s, pc_r), 0, other)

    loop(1, 8, lambda i: near_copy(i).start())
    pending.append(waits(1, 8, near_copy))
    decoder_gradients(0)
    loop(1, 8, lambda i: near_copy(i).wait_recv())
    total = picked[pl.ds(pl.multiple_of(rank(x, y, core) * 8, 8), 8), :]
    for i in range(7):
        total = total + pick_recv[i]
    by_z[z, 0] = total
    by_z[z, 1] = squares[...]
    loop(1, 8, lambda i: sum_copy(i).start())
    pending.append(waits(1, 8, sum_copy))
    decoder_gradients(1)
    loop(1, 8, lambda i: sum_copy(i).wait_recv())
    total = by_z[0]
    for i in range(1, 8):
        total = total + by_z[i]
    by_plane[core, y * 4 + x] = total
    loop(1, 16, lambda i: plane_copy(i).start())
    pending.append(waits(1, 16, plane_copy))
    decoder_gradients(2)
    loop(1, 16, lambda i: plane_copy(i).wait_recv())
    pair_copy().start()
    pending.append(pair_copy().wait_send)
    for wait in pending[:-1]:
        wait()
    pair_copy().wait_recv()
    squared = jnp.zeros((8, TILE), f32)
    for pc in range(2):
        for py in range(4):
            for px in range(4):
                at = (px % 2 + 2 * (py % 2) + 4 * pc) * 8
                grad_out[py // 2 * 2 + px // 2, at : at + 8, :] = by_plane[pc, py * 4 + px, 0]
                squared = squared + by_plane[pc, py * 4 + px, 1]
    square_out[...] = squared
    pending[-1]()


def write_kernel(staged, grad, squares, grads, grad_out, error_out, sems):
    copies = [
        pltpu.make_async_copy(staged.at[tile], grads.at[:, :, pl.ds(tile * TILE, TILE)], sems.at[tile])
        for tile in range(2 * PAIRS)
    ]
    copies.append(pltpu.make_async_copy(grad, grad_out, sems.at[2 * PAIRS]))
    for copy in copies:
        copy.start()
    for t in range(LAYERS):
        error_out[t] = jnp.sum(squares[t : t + 1, :]) * (1.0 / (TOKENS * D))
    for copy in copies:
        copy.wait()


def on_device(decoder, code_index, code_value, bias, target):
    in_vmem = pl.BlockSpec(memory_space=pltpu.VMEM)
    in_hbm = pl.BlockSpec(memory_space=pltpu.HBM)

    def sems(*dims):
        return pltpu.SemaphoreType.DMA(dims)

    errors = (PAIRS, 2, LAYERS, TOKENS, TILE)
    staged, grad, squares = pl.pallas_call(
        exchange_kernel,
        name="exchange",
        out_shape=(
            pltpu.VMEM((2 * PAIRS, SLAB, LAYERS, TILE), bf16),
            jax.ShapeDtypeStruct((LAYERS, TOPK, TOKENS), f32),
            jax.ShapeDtypeStruct((8, TILE), f32),
        ),
        in_specs=[in_hbm] * 5,
        out_specs=(in_vmem, in_vmem, in_vmem),
        scratch_shapes=[
            pltpu.VMEM((2 * PAIRS, SLAB, LAYERS, TILE), bf16),
            pltpu.VMEM((TOPK, TOKENS), jnp.int32),
            pltpu.VMEM((TOPK, TOKENS), bf16),
            pltpu.VMEM((LAYERS, D), f32),
            pltpu.VMEM((TOKENS, LAYERS * SLAB), f32),
            pltpu.VMEM((LAYERS * TOKENS, LAYERS * SLAB), bf16),
            pltpu.VMEM((PAIRS, 2, LAYERS, HALF, TILE), f32),
            pltpu.VMEM((PAIRS, 2, LAYERS, HALF, TILE), bf16),
            pltpu.VMEM((PAIRS, 2, LAYERS, HALF, TILE), bf16),
            pltpu.VMEM((PAIRS, 2, LAYERS, HALF, TILE), bf16),
            pltpu.VMEM((2, 2, ROWS, TILE), bf16),
            pltpu.VMEM((2, 3, PAIRS, LAYERS, ROWS, TILE), bf16),
            pltpu.VMEM((2, PAIRS, LAYERS, ROWS, TILE), f32),
            pltpu.VMEM((2, PAIRS, LAYERS, ROWS, TILE), bf16),
            pltpu.VMEM((2, 3, PAIRS, ROWS, TILE), bf16),
            pltpu.VMEM((2, PAIRS, ROWS, TILE), f32),
            pltpu.VMEM((8, 2, 2, ROWS, TILE), bf16),
            pltpu.VMEM((7, 2, 2, ROWS, TILE), bf16),
            pltpu.VMEM(errors, bf16),
            pltpu.VMEM((8, 2, ROWS, TILE), bf16),
            pltpu.VMEM((SLAB, TOKENS), bf16),
            pltpu.VMEM((LAYERS * SLAB, LAYERS * TOKENS), bf16),
            pltpu.VMEM((8, TILE), f32),
            pltpu.VMEM((LAYERS, LAYERS * SLAB, TOKENS), f32),
            pltpu.VMEM((SLAB, TOKENS), f32),
            pltpu.VMEM((TOPK, TOKENS), f32),
            pltpu.VMEM((7, 8, TILE), f32),
            pltpu.VMEM((8, 2, 8, TILE), f32),
            pltpu.VMEM((2, 16, 2, 8, TILE), f32),
            sems(3), sems(2 * PAIRS), sems(2, 2),
            sems(GROUPS), sems(GROUPS), sems(2, GROUPS, 3), sems(2, GROUPS, 3),
            sems(2, GROUPS, 3), sems(2, GROUPS, 3), sems(7), sems(7),
            sems(2, 3), sems(2, 3), sems(2, GROUPS, 3), sems(2, GROUPS, 3),
            sems(GROUPS), sems(GROUPS), sems(7), sems(7),
            sems(7), sems(7), sems(7), sems(7), sems(15), sems(15), sems(1), sems(1),
        ],
        compiler_params=pltpu.CompilerParams(
            collective_id=0, has_side_effects=True, vmem_limit_bytes=40 << 20
        ),
    )(
        *[
            pltpu.with_memory_space_constraint(array, pltpu.HBM)
            for array in (
                decoder,
                jnp.transpose(code_index, (0, 2, 1)),
                jnp.transpose(code_value, (0, 2, 1)),
                bias,
                target,
            )
        ]
    )
    grads, code_grad, layer_error = pl.pallas_call(
        write_kernel,
        name="write_outputs",
        out_shape=(
            jax.ShapeDtypeStruct(decoder.shape, bf16),
            jax.ShapeDtypeStruct((LAYERS, TOPK, TOKENS), f32),
            jax.ShapeDtypeStruct((LAYERS,), f32),
        ),
        in_specs=[in_vmem] * 3,
        out_specs=(in_hbm, in_hbm, pl.BlockSpec(memory_space=pltpu.SMEM)),
        scratch_shapes=[sems(2 * PAIRS + 1)],
        compiler_params=pltpu.CompilerParams(vmem_limit_bytes=8 << 20),
    )(*[pltpu.with_memory_space_constraint(array, pltpu.VMEM) for array in (staged, grad, squares)])
    return layer_error, grads, jnp.transpose(code_grad, (0, 2, 1))


def solution(mesh):
    torus = Mesh(mesh.devices.reshape(2, 4, 2, 8, 2), AXES)
    rows = P(AXES, None, None)
    return jax.shard_map(
        on_device,
        mesh=torus,
        in_specs=(rows, P(), P(), P(), P()),
        out_specs=(P(), rows, P()),
        check_vma=False,
    )
```

```python
import functools

import jax
import jax.numpy as jnp
from jax import lax
from jax.experimental import pallas as pl
from jax.experimental.pallas import tpu as pltpu
from jax.sharding import Mesh
from jax.sharding import PartitionSpec as P

D = 2304
LAYERS = 4
TOPK = 64
TOKENS = 128
SLAB = 256
TILE = 128
PAIRS = D // (2 * TILE)
GROUPS = 3
WIDE = PAIRS // GROUPS
HALF = TOKENS // 2
ROWS = 16
AXES = ("yh", "x", "core", "z", "yl")
MESH = pl.DeviceIdType.MESH
f32 = jnp.float32
bf16 = jnp.bfloat16


def contract(left, right, left_dim, right_dim):
    return lax.dot_general(
        left, right, (((left_dim,), (right_dim,)), ((), ())), preferred_element_type=f32
    )


def here():
    x, core, z = lax.axis_index("x"), lax.axis_index("core"), lax.axis_index("z")
    y = lax.axis_index("yh") * 2 + lax.axis_index("yl")
    return x, y, z, core


def source_layer():
    return lax.axis_index("yh") * 2 + lax.axis_index("x") // 2


def at_x(x):
    return {"x": x}


def at_y(y):
    return {"yh": y // 2, "yl": lax.rem(y, 2)}


def at_z(z):
    return {"z": z}


def remote(src, dst, sems, index, device):
    return pltpu.make_async_remote_copy(
        src_ref=src,
        dst_ref=dst,
        send_sem=sems[0].at[index],
        recv_sem=sems[1].at[index],
        device_id=device,
        device_id_type=MESH,
    )


def waits(low, high, copy):
    return lambda: loop(low, high, lambda i: copy(i).wait_send())


def loop(low, high, body):
    def step(i, carry):
        body(i)
        return carry

    lax.fori_loop(low, high, step, 0)


def exchange_kernel(
    decoder, index_hbm, value_hbm, bias_hbm, target,
    grads_out, grad_out, square_out,
    weights, index_ref, value_ref, bias_ref, spread_codes, forward, own, core_send, core_recv, own_b, target_v,
    recv1, sum1, sum1_b, recv2, sum2, send3, recv3,
    error, by_z_error, codes, wide_codes, squares, products, sums, picked, pick_recv, by_z, by_plane,
    small_sem, weight_sem, target_sem,
    core_s, core_r, one_s, one_r, two_s, two_r, three_s, three_r,
    as_s, as_r, af_s, af_r, ac_s, ac_r,
    az_s, az_r, pn_s, pn_r, pz_s, pz_r, pp_s, pp_r, pc_s, pc_r,
):
    x, y, z, core = here()
    source = source_layer()
    offset = ((lax.rem(x, 2) * 2 + core) * 16 + z * 2 + lax.axis_index("yl")) * SLAB
    other = {"core": 1 - core}
    pending = []
    first, second = (x, y), (y, x)
    at_first, at_second = (at_x, at_y), (at_y, at_x)
    tokens_of = [pl.multiple_of(core * HALF + first[p] * ROWS, ROWS) for p in range(2)]

    def group(g):
        return pl.ds(g * WIDE, WIDE)

    def weight_copy(tile):
        return pltpu.make_async_copy(
            decoder.at[:, :, pl.ds(tile * TILE, TILE)], weights.at[tile], weight_sem.at[tile]
        )

    def target_copy(p, which):
        tile = (z if which == 0 else PAIRS - 1) * 2 + p
        columns = pl.ds(pl.multiple_of(tile * TILE, TILE), TILE)
        return pltpu.make_async_copy(
            target.at[second[p], pl.ds(tokens_of[p], ROWS), columns],
            target_v.at[p, which],
            target_sem.at[p, which],
        )

    small = [
        pltpu.make_async_copy(index_hbm.at[source], index_ref, small_sem.at[0]),
        pltpu.make_async_copy(value_hbm.at[source], value_ref, small_sem.at[1]),
        pltpu.make_async_copy(bias_hbm, bias_ref, small_sem.at[2]),
    ]
    for copy in small:
        copy.start()
    for tile in range(2 * PAIRS):
        weight_copy(tile).start()
    for p in range(2):
        for which in range(2):
            target_copy(p, which).start()

    for b in range(PAIRS):
        for p in range(2):
            error[b, p, 0] = jnp.zeros((TOKENS, TILE), bf16)

    barrier = pltpu.get_barrier_semaphore()

    def z_peer(i):
        return lax.rem(z + i, 8)

    def at_plane(i):
        return {"x": lax.rem(x + lax.rem(i, 4), 4), **at_y(lax.rem(y + i // 4, 4))}

    def flip(position, by):
        return position + by * (1 - 2 * lax.rem(position, 2))

    def near(i):
        return flip(x, lax.rem(i, 2)), flip(y, lax.rem(i // 2, 2)), flip(core, i // 4)

    def at_near(i):
        px, py, pc = near(i)
        return {"x": px, "core": pc, **at_y(py)}

    def greet(device):
        pl.semaphore_signal(barrier, inc=1, device_id=device, device_id_type=MESH)

    loop(1, 8, lambda i: greet(at_z(z_peer(i))))
    loop(1, 16, lambda i: greet(at_plane(i)))
    loop(4, 8, lambda i: greet(at_near(i)))

    for copy in small:
        copy.wait()
    latents = lax.broadcasted_iota(jnp.int32, (SLAB, TOKENS), 0)

    def place(i, dense):
        part = pl.ds(pl.multiple_of(i * ROWS, ROWS), ROWS)
        columns = index_ref[part, :] - offset
        values = value_ref[part, :].astype(f32)
        for k in range(ROWS):
            dense = jnp.where(latents == columns[k : k + 1, :], values[k : k + 1, :], dense)
        return dense

    dense = lax.fori_loop(0, TOPK // ROWS, place, jnp.zeros((SLAB, TOKENS), f32)).astype(bf16)
    codes[...] = dense
    lane = lax.broadcasted_iota(jnp.int32, (SLAB, LAYERS * SLAB), 1)
    row = lax.broadcasted_iota(jnp.int32, (SLAB, LAYERS * SLAB), 0)
    spread = jnp.where((lane >> 2) == row, 1.0, 0.0).astype(bf16)
    spread_codes[...] = contract(dense, spread, 0, 0)
    lane = lax.broadcasted_iota(jnp.int32, (HALF, LAYERS * SLAB), 1) & 3
    for side in range(2):
        half = spread_codes[pl.ds(pl.multiple_of((core if side == 0 else 1 - core) * HALF, HALF), HALF), :]
        for t in range(LAYERS):
            kept = jnp.where(jnp.logical_and(lane == t, t >= source), half, 0.0)
            forward[(side * LAYERS + t) * HALF : (side * LAYERS + t + 1) * HALF, :] = kept.astype(bf16)

    flat = weights.reshape(2 * PAIRS, LAYERS * SLAB, TILE)

    def core_copy(g):
        return remote(core_send.at[group(g)], core_recv.at[group(g)], (core_s, core_r), g, other)

    def layers(low):
        return pl.ds(low, LAYERS - low)

    def one_copy(low, g, p, i):
        k = lax.rem(first[p] + i, 4)
        rows = pl.ds(pl.multiple_of(k * ROWS, ROWS), ROWS)
        return remote(
            own_b.at[group(g), p, layers(low), rows, :], recv1.at[p, i - 1, group(g), layers(low)],
            (one_s, one_r), (p, g, i - 1), at_first[p](k),
        )

    def two_copy(g, p, i):
        k = lax.rem(second[p] + i, 4)
        return remote(
            sum1_b.at[p, group(g), k], recv2.at[p, i - 1, group(g)],
            (two_s, two_r), (p, g, i - 1), at_second[p](k),
        )

    def three_copy(i):
        return remote(send3.at[z_peer(i)], recv3.at[i - 1], (three_s, three_r), i - 1, at_z(z_peer(i)))

    def z_copy(i):
        return remote(by_z_error.at[z], by_z_error.at[z], (az_s, az_r), i - 1, at_z(z_peer(i)))

    def second_copy(p, i):
        tiles = error.at[:, p, second[p], pl.ds(tokens_of[p], ROWS), :]
        return remote(tiles, tiles, (as_s, as_r), (p, i - 1), at_second[p](lax.rem(second[p] + i, 4)))

    def first_copy(low, g, p, i):
        tiles = error.at[group(g), p, layers(low), pl.ds(tokens_of[p], ROWS), :]
        return remote(tiles, tiles, (af_s, af_r), (p, g, i - 1), at_first[p](lax.rem(first[p] + i, 4)))

    def half_copy(g):
        tiles = error.at[group(g), :, :, pl.ds(pl.multiple_of(core * HALF, HALF), HALF), :]
        return remote(tiles, tiles, (ac_s, ac_r), g, other)

    def no_source(p, position):
        across = lax.axis_index("yh") if p == 0 else lax.axis_index("x") // 2
        return jnp.logical_or(across > 0, position > 1)

    def either(late, do):
        @pl.when(late)
        def _():
            do(1)

        @pl.when(jnp.logical_not(late))
        def _():
            do(0)

    def one_start(g, p, i):
        either(source > 0, lambda low: one_copy(low, g, p, i).start())
        pending.append(lambda: either(source > 0, lambda low: one_copy(low, g, p, i).wait_send()))

    def one_arrive(g, p, i):
        late = no_source(p, lax.rem(first[p] + 4 - i, 4))
        either(late, lambda low: one_copy(low, g, p, i).wait_recv())

    def first_start(g, p, i):
        late = no_source(p, lax.rem(first[p] + i, 4))
        either(late, lambda low: first_copy(low, g, p, i).start())
        pending.append(lambda: either(late, lambda low: first_copy(low, g, p, i).wait_send()))

    def first_arrive(g, p, i):
        either(source > 0, lambda low: first_copy(low, g, p, i).wait_recv())

    def exchange(copy, g):
        for i in range(1, 4):
            for p in range(2):
                copy(g, p, i).start()
                pending.append(copy(g, p, i).wait_send)

    def arrive(copy, g):
        for p in range(2):
            for i in range(1, 4):
                copy(g, p, i).wait_recv()

    layer_of = lax.broadcasted_iota(jnp.int32, (LAYERS, ROWS, TILE), 0)

    def add_core(g):
        core_copy(g).wait_recv()

        def add(i):
            b, p = g * WIDE + i // 2, lax.rem(i, 2)
            total = own[b, p] + core_recv[b, p].astype(f32)
            own[b, p] = total
            own_b[b, p] = total.astype(bf16)

        loop(0, 2 * WIDE, add)
        for i in range(1, 4):
            for p in range(2):
                one_start(g, p, i)

    def add_first(g):
        for p in range(2):
            for i in range(1, 4):
                one_arrive(g, p, i)
        for p in range(2):

            def add(b):
                total = own[b, p, :, pl.ds(pl.multiple_of(first[p] * ROWS, ROWS), ROWS), :]
                for i in range(3):
                    part = recv1[p, i, b].astype(f32)
                    late = no_source(p, lax.rem(first[p] + 3 - i, 4))
                    total = total + jnp.where(jnp.logical_and(late, layer_of == 0), 0.0, part)
                sum1[p, b] = total
                sum1_b[p, b] = total.astype(bf16)

            loop(g * WIDE, (g + 1) * WIDE, add)
        exchange(two_copy, g)

    def add_second(g):
        arrive(two_copy, g)
        for p in range(2):

            for b in range(g * WIDE, (g + 1) * WIDE):
                total = sum1[p, b, second[p]]
                for k in range(3):
                    total = total + recv2[p, k, b].astype(f32)
                sum2[p, b] = total
                if b < 8:
                    send3[b, 0, p] = total.astype(bf16)
                else:
                    for k in range(8):
                        send3[k, 1, p] = total.astype(bf16)

    def add_z():
        loop(1, 8, lambda i: three_copy(i).start())
        pending.append(waits(1, 8, three_copy))

    layer_row = lax.broadcasted_iota(jnp.int32, (LAYERS, TILE), 0)
    tile_row = lax.broadcasted_iota(jnp.int32, (8, TILE), 0)

    def take_errors():
        squared = jnp.zeros((8, TILE), f32)
        loop(1, 8, lambda i: three_copy(i).wait_recv())
        for which in range(2):
            for p in range(2):
                target_copy(p, which).wait()
                tile = z if which == 0 else PAIRS - 1
                total = sum2[p, tile]
                for i in range(7):
                    total = total + recv3[i, which, p].astype(f32)
                columns = pl.ds(pl.multiple_of((tile * 2 + p) * TILE, TILE), TILE)
                shift = jnp.sum(jnp.where(layer_row == second[p], bias_ref[:, columns], 0.0), axis=0, keepdims=True)
                residual = total + shift - target_v[p, which].astype(f32)
                if which == 0:
                    by_z_error[z, p] = residual.astype(bf16)
                else:
                    error[tile, p, second[p], pl.ds(tokens_of[p], ROWS), :] = residual.astype(bf16)
                square = jnp.sum(residual * residual, axis=0, keepdims=True)
                counted = tile_row == second[p]
                if which == 1:
                    counted = jnp.logical_and(counted, z == 0)
                squared = squared + jnp.where(counted, square, 0.0)
            if which == 0:
                loop(1, 8, lambda i: z_copy(i).start())
                pending.append(waits(1, 8, z_copy))
        squares[...] = squared

    def pass_layers():
        loop(1, 8, lambda i: z_copy(i).wait_recv())
        for p in range(2):
            for b in range(8):
                error[b, p, second[p], pl.ds(tokens_of[p], ROWS), :] = by_z_error[b, p]
            for i in range(1, 4):
                second_copy(p, i).start()
                pending.append(second_copy(p, i).wait_send)
        for p in range(2):
            for i in range(1, 4):
                second_copy(p, i).wait_recv()

    def pass_rows(g):
        for p in range(2):
            for i in range(1, 4):
                first_arrive(g, p, i)
        half_copy(g).start()
        pending.append(half_copy(g).wait_send)

    def backward(g):
        half_copy(g).wait_recv()
        left, right = [], []
        for b in range(g * WIDE, (g + 1) * WIDE):
            for p in range(2):
                left.append(flat[2 * b + p])
                right.append(error[b, p].reshape(LAYERS * TOKENS, TILE))
        product = contract(jnp.concatenate(left, axis=1), jnp.concatenate(right, axis=1), 1, 1)
        for t in range(LAYERS):
            block = product[:, t * TILE : (t + 1) * TILE]
            products[t] = block if g == 0 else products[t] + block

    def project(g):
        for tile in range(2 * g * WIDE, 2 * (g + 1) * WIDE):
            weight_copy(tile).wait()
        tiles = [flat[tile] for tile in range(2 * g * WIDE, 2 * (g + 1) * WIDE)]
        product = contract(forward[...], jnp.concatenate(tiles, axis=1), 1, 0)
        for i in range(WIDE):
            b = g * WIDE + i
            for p in range(2):
                columns = slice((2 * i + p) * TILE, (2 * i + p + 1) * TILE)
                own[b, p] = product[: LAYERS * HALF, columns].reshape(LAYERS, HALF, TILE)
                core_send[b, p] = product[LAYERS * HALF :, columns].reshape(LAYERS, HALF, TILE).astype(bf16)

    def send_core(g):
        core_copy(g).start()
        pending.append(core_copy(g).wait_send)

    project(0)
    project(1)
    pl.semaphore_wait(barrier, 26)
    send_core(0)
    send_core(1)
    project(2)
    send_core(2)
    for stage in (add_core, add_first, add_second):
        for g in range(GROUPS):
            stage(g)
    add_z()
    pattern_row = lax.broadcasted_iota(jnp.int32, (LAYERS * SLAB, SLAB), 0)
    pattern_lane = lax.broadcasted_iota(jnp.int32, (LAYERS * SLAB, SLAB), 1)
    pattern = jnp.where((pattern_row >> 2) == pattern_lane, 1.0, 0.0).astype(bf16)
    tall = contract(pattern, codes[...], 1, 0)
    pattern_row = lax.broadcasted_iota(jnp.int32, (LAYERS * SLAB, TOKENS), 0) & 3
    for t in range(LAYERS):
        kept = jnp.where(jnp.logical_and(pattern_row == t, t >= source), tall, 0.0)
        wide_codes[:, t * TOKENS : (t + 1) * TOKENS] = kept.astype(bf16)
    take_errors()
    pass_layers()
    for g in range(GROUPS):
        for i in range(1, 4):
            for p in range(2):
                first_start(g, p, i)
    for g in range(GROUPS):
        pass_rows(g)
        if g > 0:
            backward(g - 1)
    backward(GROUPS - 1)

    total = jnp.zeros((SLAB, TOKENS), f32)
    for t in range(LAYERS):
        total = total + jnp.where(t >= source, products[t, pl.ds(t, SLAB, stride=LAYERS), :], 0.0)
    sums[...] = total
    columns = index_ref[...] - offset

    def pick(i, out):
        rows = sums[pl.ds(pl.multiple_of(i * 8, 8), 8), :]
        for r in range(8):
            out = jnp.where(columns == i * 8 + r, rows[r : r + 1, :], out)
        return out

    picked[...] = lax.fori_loop(0, SLAB // 8, pick, jnp.zeros((TOPK, TOKENS), f32))

    flat_out = grads_out.reshape(2 * PAIRS, LAYERS * SLAB, TILE)

    def decoder_gradients(g):
        tiles = range(2 * g * WIDE, 2 * (g + 1) * WIDE)
        errors = [error[tile // 2, tile % 2].reshape(LAYERS * TOKENS, TILE) for tile in tiles]
        product = contract(wide_codes[...], jnp.concatenate(errors, axis=1), 1, 0).astype(bf16)
        for i, tile in enumerate(tiles):
            flat_out[tile] = product[:, i * TILE : (i + 1) * TILE]

    def rank(px, py, pc):
        return lax.rem(px, 2) + 2 * lax.rem(py, 2) + 4 * pc

    def near_copy(i):
        rows = picked.at[pl.ds(pl.multiple_of(rank(*near(i)) * 8, 8), 8), :]
        return remote(rows, pick_recv.at[i - 1], (pn_s, pn_r), i - 1, at_near(i))

    def sum_copy(i):
        return remote(by_z.at[z], by_z.at[z], (pz_s, pz_r), i - 1, at_z(z_peer(i)))

    def plane_copy(i):
        mine = by_plane.at[core, y * 4 + x]
        return remote(mine, mine, (pp_s, pp_r), i - 1, at_plane(i))

    def pair_copy():
        return remote(by_plane.at[core], by_plane.at[core], (pc_s, pc_r), 0, other)

    loop(1, 8, lambda i: near_copy(i).start())
    pending.append(waits(1, 8, near_copy))
    decoder_gradients(0)
    loop(1, 8, lambda i: near_copy(i).wait_recv())
    total = picked[pl.ds(pl.multiple_of(rank(x, y, core) * 8, 8), 8), :]
    for i in range(7):
        total = total + pick_recv[i]
    by_z[z, 0] = total
    by_z[z, 1] = squares[...]
    loop(1, 8, lambda i: sum_copy(i).start())
    pending.append(waits(1, 8, sum_copy))
    decoder_gradients(1)
    loop(1, 8, lambda i: sum_copy(i).wait_recv())
    total = by_z[0]
    for i in range(1, 8):
        total = total + by_z[i]
    by_plane[core, y * 4 + x] = total
    loop(1, 16, lambda i: plane_copy(i).start())
    pending.append(waits(1, 16, plane_copy))
    decoder_gradients(2)
    loop(1, 16, lambda i: plane_copy(i).wait_recv())
    pair_copy().start()
    pending.append(pair_copy().wait_send)
    for wait in pending[:-1]:
        wait()
    pair_copy().wait_recv()
    squared = jnp.zeros((8, TILE), f32)
    for pc in range(2):
        for py in range(4):
            for px in range(4):
                at = (px % 2 + 2 * (py % 2) + 4 * pc) * 8
                grad_out[py // 2 * 2 + px // 2, at : at + 8, :] = by_plane[pc, py * 4 + px, 0]
                squared = squared + by_plane[pc, py * 4 + px, 1]
    square_out[...] = squared
    pending[-1]()


def write_kernel(staged, grad, squares, grads, grad_out, error_out, sems):
    copies = [
        pltpu.make_async_copy(staged.at[tile], grads.at[:, :, pl.ds(tile * TILE, TILE)], sems.at[tile])
        for tile in range(2 * PAIRS)
    ]
    copies.append(pltpu.make_async_copy(grad, grad_out, sems.at[2 * PAIRS]))
    for copy in copies:
        copy.start()
    for t in range(LAYERS):
        error_out[t] = jnp.sum(squares[t : t + 1, :]) * (1.0 / (TOKENS * D))
    for copy in copies:
        copy.wait()


def on_device(decoder, code_index, code_value, bias, target):
    in_vmem = pl.BlockSpec(memory_space=pltpu.VMEM)
    in_hbm = pl.BlockSpec(memory_space=pltpu.HBM)

    def sems(*dims):
        return pltpu.SemaphoreType.DMA(dims)

    errors = (PAIRS, 2, LAYERS, TOKENS, TILE)
    staged, grad, squares = pl.pallas_call(
        exchange_kernel,
        name="exchange",
        out_shape=(
            pltpu.VMEM((2 * PAIRS, SLAB, LAYERS, TILE), bf16),
            jax.ShapeDtypeStruct((LAYERS, TOPK, TOKENS), f32),
            jax.ShapeDtypeStruct((8, TILE), f32),
        ),
        in_specs=[in_hbm] * 5,
        out_specs=(in_vmem, in_vmem, in_vmem),
        scratch_shapes=[
            pltpu.VMEM((2 * PAIRS, SLAB, LAYERS, TILE), bf16),
            pltpu.VMEM((TOPK, TOKENS), jnp.int32),
            pltpu.VMEM((TOPK, TOKENS), bf16),
            pltpu.VMEM((LAYERS, D), f32),
            pltpu.VMEM((TOKENS, LAYERS * SLAB), f32),
            pltpu.VMEM((LAYERS * TOKENS, LAYERS * SLAB), bf16),
            pltpu.VMEM((PAIRS, 2, LAYERS, HALF, TILE), f32),
            pltpu.VMEM((PAIRS, 2, LAYERS, HALF, TILE), bf16),
            pltpu.VMEM((PAIRS, 2, LAYERS, HALF, TILE), bf16),
            pltpu.VMEM((PAIRS, 2, LAYERS, HALF, TILE), bf16),
            pltpu.VMEM((2, 2, ROWS, TILE), bf16),
            pltpu.VMEM((2, 3, PAIRS, LAYERS, ROWS, TILE), bf16),
            pltpu.VMEM((2, PAIRS, LAYERS, ROWS, TILE), f32),
            pltpu.VMEM((2, PAIRS, LAYERS, ROWS, TILE), bf16),
            pltpu.VMEM((2, 3, PAIRS, ROWS, TILE), bf16),
            pltpu.VMEM((2, PAIRS, ROWS, TILE), f32),
            pltpu.VMEM((8, 2, 2, ROWS, TILE), bf16),
            pltpu.VMEM((7, 2, 2, ROWS, TILE), bf16),
            pltpu.VMEM(errors, bf16),
            pltpu.VMEM((8, 2, ROWS, TILE), bf16),
            pltpu.VMEM((SLAB, TOKENS), bf16),
            pltpu.VMEM((LAYERS * SLAB, LAYERS * TOKENS), bf16),
            pltpu.VMEM((8, TILE), f32),
            pltpu.VMEM((LAYERS, LAYERS * SLAB, TOKENS), f32),
            pltpu.VMEM((SLAB, TOKENS), f32),
            pltpu.VMEM((TOPK, TOKENS), f32),
            pltpu.VMEM((7, 8, TILE), f32),
            pltpu.VMEM((8, 2, 8, TILE), f32),
            pltpu.VMEM((2, 16, 2, 8, TILE), f32),
            sems(3), sems(2 * PAIRS), sems(2, 2),
            sems(GROUPS), sems(GROUPS), sems(2, GROUPS, 3), sems(2, GROUPS, 3),
            sems(2, GROUPS, 3), sems(2, GROUPS, 3), sems(7), sems(7),
            sems(2, 3), sems(2, 3), sems(2, GROUPS, 3), sems(2, GROUPS, 3),
            sems(GROUPS), sems(GROUPS), sems(7), sems(7),
            sems(7), sems(7), sems(7), sems(7), sems(15), sems(15), sems(1), sems(1),
        ],
        compiler_params=pltpu.CompilerParams(
            collective_id=0, has_side_effects=True, vmem_limit_bytes=40 << 20
        ),
    )(
        *[
            pltpu.with_memory_space_constraint(array, pltpu.HBM)
            for array in (
                decoder,
                jnp.transpose(code_index, (0, 2, 1)),
                jnp.transpose(code_value, (0, 2, 1)),
                bias,
                target,
            )
        ]
    )
    grads, code_grad, layer_error = pl.pallas_call(
        write_kernel,
        name="write_outputs",
        out_shape=(
            jax.ShapeDtypeStruct(decoder.shape, bf16),
            jax.ShapeDtypeStruct((LAYERS, TOPK, TOKENS), f32),
            jax.ShapeDtypeStruct((LAYERS,), f32),
        ),
        in_specs=[in_vmem] * 3,
        out_specs=(in_hbm, in_hbm, pl.BlockSpec(memory_space=pltpu.SMEM)),
        scratch_shapes=[sems(2 * PAIRS + 1)],
        compiler_params=pltpu.CompilerParams(vmem_limit_bytes=8 << 20),
    )(*[pltpu.with_memory_space_constraint(array, pltpu.VMEM) for array in (staged, grad, squares)])
    return layer_error, grads, jnp.transpose(code_grad, (0, 2, 1))


def solution(mesh):
    torus = Mesh(mesh.devices.reshape(2, 4, 2, 8, 2), AXES)
    rows = P(AXES, None, None)
    return jax.shard_map(
        on_device,
        mesh=torus,
        in_specs=(rows, P(), P(), P(), P()),
        out_specs=(P(), rows, P()),
        check_vma=False,
    )
```
